32 devices in a mesh: dp: 8 (over y, x, core), vis: 4 (over z).
Axes of the slice: x: 2, y: 2, z: 4, core: 2. Of those that a mesh axis runs over, the one named last changes fastest.
Arguments:
- patches: bfloat16 [16384, 1280], P(('dp', 'vis')), may hold values from -100 to 100
- window_index: int32 [32, 512], P(('dp', 'vis')), may hold values from 0 to 511, each once within a row
- window_live: int32 [32, 8], P(('dp', 'vis')), may hold values from 0 to 64, as said below
- d_merged: bfloat16 [4096, 5120], P(('dp', 'vis')), may hold values from -1 to 1
- w_qkv: bfloat16 [1280, 2880], replicated, may hold values from -20 to 20
- w_out: bfloat16 [960, 1280], replicated, may hold values from -0.1875 to 0.1875
- merge_gain: float32 [1280], replicated, may hold values from 0.1 to 1.9
Outputs:
- merged: bfloat16 [4096, 5120], P(('dp', 'vis'))
- grad_qkv: float32 [1280, 2880], P(('dp', 'vis'))
- grad_out: float32 [960, 1280], P(None, ('dp', 'vis'))
- grad_gain: float32 [1280], P(('dp', 'vis'))
The draws below stay inside these ranges and needn't reach their ends.
Inputs may be any that keep to these rules, and one draw needn't show every extreme that they name: `window_live`: entry [i, w] gives the live rows of window slot w of device i = dp * 4 + vis: 0 for an empty slot, else a multiple of 4. On every device the slots with live rows come first. In every vis column the 8 owners hold together exactly 32 windows with live rows.
All inputs are finite; a program needn't handle non-finite values.
Results may differ from the reference program's by a relative error of at most 0.018.
Values may be sent and summed in bfloat16 or wider, within the bound.
No kernel may reach another device: no remote copies, remote signals or barrier semaphores. Data moves between devices by JAX's collectives and lax.ppermute only.
A program may use at most 192 MiB of HBM per device.

```python
import math
import jax
import jax.numpy as jnp
from jax import lax

D = 1280
HEADS = 12
HEAD_DIM = 80
WIN = 64
W_DEV = 8
N_DP = 8
N_VIS = 4


def draw_patches(key, part):
    key = jax.random.fold_in(key, 11)
    first_key, second_key, third_key = jax.random.split(key, 3)
    total_rows = N_DP * N_VIS * W_DEV * WIN
    row_scale = 0.3 * jnp.exp(jax.random.uniform(second_key, (total_rows, 1), jnp.float32, 0.0, math.log(10.0)))
    col_scale = 0.3 * jnp.exp(jax.random.uniform(third_key, (1, D), jnp.float32, 0.0, math.log(10.0)))
    base = jnp.clip(jax.random.normal(first_key, (total_rows, D), jnp.float32), -6.0, 6.0)
    return (base * row_scale * 3.0 * col_scale * 3.0 * 0.1).astype(jnp.bfloat16)


def draw_d_merged(key, part):
    key = jax.random.fold_in(key, 17)
    total_rows = N_DP * N_VIS * W_DEV * WIN
    shape_out = (total_rows // 4, 4 * D)
    factor = total_rows ** (-0.5)
    base = jnp.clip(jax.random.normal(key, shape_out, jnp.float32), -6.0, 6.0)
    return (base * factor).astype(jnp.bfloat16)


def draw_w_qkv(key, part):
    key = jax.random.fold_in(key, 23)
    first_key = jax.random.fold_in(key, 0)
    inner_width = HEADS * HEAD_DIM
    full = jnp.clip(jax.random.normal(first_key, (D, 3 * inner_width), jnp.float32), -6.0, 6.0) * D ** (-0.5)
    return full.astype(jnp.bfloat16)


def draw_window_live(key, part):
    key = jax.random.fold_in(key, 5)
    keys_all = jax.random.split(key, 4)
    half_ranks = N_DP // 2
    split_at = jax.random.randint(keys_all[0], (N_VIS, half_ranks), 0, W_DEV + 1)
    split_at = split_at.at[:, 0].set(W_DEV)
    counts = jnp.concatenate([split_at, W_DEV - split_at], axis=1)
    orders = jax.vmap(lambda one_key: jax.random.permutation(one_key, N_DP))(jax.random.split(keys_all[1], N_VIS))
    counts = jnp.take_along_axis(counts, orders, axis=1)
    fully = jax.random.randint(keys_all[2], (N_VIS, N_DP, W_DEV), 0, 4) > 0
    partly = 4 * jax.random.randint(keys_all[3], (N_VIS, N_DP, W_DEV), 1, WIN // 4)
    live_rows = jnp.where(fully, WIN, partly)
    slot_ids = jnp.arange(W_DEV, dtype=jnp.int32)
    live_rows = jnp.where(slot_ids[None, None, :] < counts[:, :, None], live_rows, 0)
    forced = (counts[:, :, None] == W_DEV) & (slot_ids[None, None, :] == 0)
    live_rows = jnp.where(forced, WIN, live_rows)
    return jnp.transpose(live_rows, (1, 0, 2)).reshape(N_DP * N_VIS, W_DEV).astype(jnp.int32)


def bell_draw(stream_key, dims, spread, most, kind=jnp.bfloat16):
    drawn = jax.random.normal(stream_key, dims, jnp.float32) * spread
    return jnp.minimum(jnp.maximum(drawn, -most), most).astype(kind)


def setup_inputs(seed: int = 0) -> dict:
    streams_of = jax.random.split(jax.random.key(seed), 8)
    return {
        "patches": draw_patches(jax.random.fold_in(streams_of[7], 71), 0),
        "window_index": jax.vmap(lambda own: jax.random.permutation(own, W_DEV * WIN))(jax.random.split(streams_of[1], (N_DP * N_VIS))).reshape((N_DP * N_VIS, W_DEV * WIN)).astype(jnp.int32),
        "window_live": draw_window_live(jax.random.fold_in(streams_of[7], 71), 0),
        "d_merged": draw_d_merged(jax.random.fold_in(streams_of[7], 71), 0),
        "w_qkv": draw_w_qkv(jax.random.fold_in(streams_of[7], 71), 0),
        "w_out": bell_draw(streams_of[5], (HEADS * HEAD_DIM, D), (HEADS * HEAD_DIM) ** -0.5, 0.1875),
        "merge_gain": jnp.clip(1.0 + 0.18 * jax.random.normal(streams_of[6], (D,), jnp.float32), 0.1, 1.9),
    }


EPSILON = 1e-06
NEGATIVE = -1e+30

def contract(formula, first_op, second_op):
    return jnp.einsum(formula, first_op.astype(jnp.float32), second_op.astype(jnp.float32))

def lower(values_in):
    return lax.optimization_barrier(values_in.astype(jnp.bfloat16))

def forward(window_rows, live_rows, w_qkv, w_out, merge_gain):
    window_count, win_rows, model_width = window_rows.shape
    inner_width = w_out.shape[0]
    head_width = inner_width // HEADS
    widened = window_rows.astype(jnp.float32)
    normed = lower(widened * lax.rsqrt(lax.optimization_barrier(jnp.mean(widened * widened, -1, keepdims=True)) + EPSILON))
    packed = lower(contract('bwd,de->bwe', normed, w_qkv))
    packed = packed.reshape(window_count, win_rows, 3, HEADS, head_width)
    query = packed[:, :, 0]
    key_rows = packed[:, :, 1]
    values = packed[:, :, 2]
    scores = contract('bqhc,bkhc->bhqk', query, key_rows) * head_width ** (-0.5)
    alive = jnp.arange(win_rows)[None, :] < live_rows[:, None]
    scores = jnp.where(alive[:, None, None, :], scores, NEGATIVE)
    probs = jax.nn.softmax(scores, axis=-1)
    probs_low = lower(probs)
    context = lower(contract('bhqk,bkhc->bqhc', probs_low, values)).reshape(window_count, win_rows, inner_width)
    attended = widened + contract('bwi,id->bwd', context, w_out)
    inverse = lax.rsqrt(lax.optimization_barrier(jnp.mean(attended * attended, -1, keepdims=True)) + EPSILON)
    normalized = attended * inverse
    row_mask = alive[:, :, None].astype(jnp.float32)
    merged = (normalized * merge_gain * row_mask).astype(jnp.bfloat16).reshape(window_count, win_rows // 4, 4 * model_width)
    saved = (normed, query, key_rows, values, probs, probs_low, context, normalized, inverse, row_mask)
    return (merged, saved)

def backward(saved, cotangent, w_out, merge_gain):
    normed, query, key_rows, values, probs, probs_low, context, normalized, inverse, row_mask = saved
    window_count, win_rows, model_width = normalized.shape
    head_width = query.shape[-1]
    grad_rows = cotangent.astype(jnp.float32).reshape(window_count, win_rows, model_width) * row_mask
    grad_gain = lax.optimization_barrier(jnp.sum(grad_rows * normalized, axis=(0, 1)))
    scaled = grad_rows * merge_gain
    d_attended = lower(inverse * (scaled - normalized * lax.optimization_barrier(jnp.mean(scaled * normalized, -1, keepdims=True))))
    grad_out = contract('bwi,bwd->id', context, d_attended)
    d_context = lower(contract('bwd,id->bwi', d_attended, w_out)).reshape(window_count, win_rows, HEADS, head_width)
    d_values = contract('bhqk,bqhc->bkhc', probs_low, d_context)
    d_probs = contract('bqhc,bkhc->bhqk', d_context, values)
    d_scores = lower(probs * (d_probs - lax.optimization_barrier(jnp.sum(d_probs * probs, -1, keepdims=True))) * head_width ** (-0.5))
    d_query = contract('bhqk,bkhc->bqhc', d_scores, key_rows)
    d_keys = contract('bhqk,bqhc->bkhc', d_scores, query)
    d_packed = lower(jnp.stack([d_query, d_keys, d_values], axis=2)).reshape(window_count, win_rows, -1)
    grad_qkv = contract('bwd,bwe->de', normed, d_packed)
    return (grad_qkv, grad_out, grad_gain)

def reference(patches, window_index, window_live, d_merged, w_qkv, w_out, merge_gain):
    device_count = N_DP * N_VIS
    block_rows = patches.reshape(device_count, W_DEV * WIN, D)
    cot_blocks = d_merged.reshape(device_count, W_DEV, WIN // 4, 4 * D)
    inner_width = HEADS * HEAD_DIM

    def step(carry, pieces):
        block, order, live_rows, cot_block = pieces
        window_rows = jnp.take(block, order.astype(jnp.int32), axis=0).reshape(W_DEV, WIN, D)
        merged, saved = forward(window_rows, live_rows, w_qkv, w_out, merge_gain)
        grad_qkv, grad_out, grad_gain = backward(saved, cot_block, w_out, merge_gain)
        return ((carry[0] + grad_qkv, carry[1] + grad_out, carry[2] + grad_gain), merged)
    start = (jnp.zeros((D, 3 * inner_width), jnp.float32), jnp.zeros((inner_width, D), jnp.float32), jnp.zeros((D,), jnp.float32))
    totals, merged = lax.scan(step, start, (block_rows, window_index, window_live, cot_blocks))
    return (merged.reshape(device_count * W_DEV * (WIN // 4), 4 * D), totals[0], totals[1], totals[2])
```

```python
import functools

import jax
import jax.numpy as jnp
from jax import lax
from jax.experimental import pallas as pl
from jax.experimental.pallas import tpu as pltpu
from jax.sharding import PartitionSpec as P

HEADS = 12
STAGE = 4
PARTS = 3
JOIN = 4
PAIR = 2
LANES = 128
TILE = 256
EPSILON = 1e-06
NEGATIVE = -1e30
F32 = jnp.float32
BF16 = jnp.bfloat16


def ceil_to(size, step):
    return -(-size // step) * step


def dot(left, right, left_axis=1, right_axis=0):
    return lax.dot_general(
        left, right, (((left_axis,), (right_axis,)), ((), ())), preferred_element_type=F32
    )


def tiles(width, step=TILE):
    return [(at, min(step, width - at)) for at in range(0, width, step)]


def alive_of(place, live_first, live_second, group):
    limit = jnp.where((place // group) % PAIR == 0, live_first, live_second)
    return (place % group) * JOIN < limit


def forward_kernel(
    rank_ref, live_ref, index_ref, patches_ref, gain_ref, cot_hbm, w_qkv_hbm, w_out_hbm,
    merged_hbm, packed_hbm, probs_hbm, d_context_hbm, context_hbm,
    norm_keep_hbm, norm_send_hbm, att_keep_hbm, att_send_hbm,
    cot_ref, w_qkv_ref, w_out_ref,
    merged_ref, packed_ref, probs_ref, d_context_ref, context_ref,
    norm_keep_ref, norm_send_ref, att_keep_ref, att_send_ref,
    rows_ref, norm_ref, turned_ref, upright_ref, d_att_ref, gain_sum_ref, place_ref, chosen_ref,
    in_sems, out_sems,
):
    row_count, model_width = patches_ref.shape
    inner = w_out_ref.shape[0]
    head_width = inner // HEADS
    slots = live_ref.shape[1]
    win_rows = row_count // slots
    group = win_rows // JOIN
    block = PAIR * win_rows
    strip = PAIR * group
    pairs = slots // PAIR
    scale = head_width ** (-0.5)
    outs = {}

    parts = tiles(3 * inner, inner // 2)
    loads = [
        pltpu.make_async_copy(
            w_qkv_hbm.at[pl.ds(at, size)], w_qkv_ref.at[pl.ds(at, size)], in_sems.at[n]
        )
        for n, (at, size) in enumerate(parts)
    ]
    load_out = pltpu.make_async_copy(w_out_hbm, w_out_ref, in_sems.at[len(parts)])
    load_cot = pltpu.make_async_copy(cot_hbm, cot_ref, in_sems.at[len(parts) + 1])
    for load in loads + [load_out, load_cot]:
        load.start()

    def give(n, source, target):
        outs[n] = pltpu.make_async_copy(source, target, out_sems.at[n])
        outs[n].start()

    def by_core(source, keep, send):
        half, rank_rows, _ = keep.shape
        core, chip = rank_ref[0] & 1, rank_ref[0] >> 1
        for rank in range(2 * half):
            piece = source[rank * rank_rows:(rank + 1) * rank_rows, :]

            @pl.when(core == rank % 2)
            def _():
                keep[chip ^ (rank // 2)] = piece

            @pl.when(core != rank % 2)
            def _():
                send[chip ^ (rank // 2)] = piece

    places = jnp.broadcast_to(index_ref[...].astype(F32), (LANES, row_count))
    place_ref[...] = places.T
    raster = lax.broadcasted_iota(jnp.int32, (strip, row_count), 1)
    for pair in range(pairs):
        for turn in range(JOIN):
            at = pair * block + turn * strip
            place = place_ref[pl.ds(pair * block + turn, strip, stride=JOIN), :]
            found = raster == place[:, :1].astype(jnp.int32)
            chosen_ref[at:at + strip, :] = jnp.where(found, 1.0, 0.0).astype(BF16)
    for at, size in tiles(model_width):
        rows_ref[:, at:at + size] = dot(chosen_ref[...], patches_ref[:, at:at + size])

    for pair in range(pairs):
        here = slice(pair * block, (pair + 1) * block)
        rows = rows_ref[here, :]
        power = jnp.mean(rows * rows, axis=1, keepdims=True)
        normed = (rows * lax.rsqrt(power + EPSILON)).astype(BF16)
        norm_ref[:, here] = normed.T
    by_core(norm_ref, norm_keep_ref, norm_send_ref)
    give(0, norm_keep_ref, norm_keep_hbm)
    give(1, norm_send_ref, norm_send_hbm)

    for load, (first, height) in zip(loads, parts):
        load.wait()
        for at, size in tiles(height):
            at += first
            found = dot(w_qkv_ref[at:at + size, :], norm_ref[...]).astype(BF16)
            part, at = at // inner, at % inner
            for pair in range(pairs):
                packed_ref[pair, part, at:at + size, :] = found[:, pair * block:(pair + 1) * block]
    give(2, packed_ref, packed_hbm)

    @pl.loop(0, pairs)
    def _(pair):
        here = pl.ds(pl.multiple_of(pair * block, block), block)
        key_at = lax.broadcasted_iota(jnp.int32, (block, block), 0)
        query_at = lax.broadcasted_iota(jnp.int32, (block, block), 1)
        allowed = alive_of(key_at, live_ref[0, PAIR * pair], live_ref[0, PAIR * pair + 1], group)
        allowed = allowed & ((key_at // group) % PAIR == (query_at // group) % PAIR)
        for first in range(0, HEADS, STAGE):
            spans = [
                slice(head * head_width, (head + 1) * head_width)
                for head in range(first, first + STAGE)
            ]
            scores = [
                dot(packed_ref[pair, 1, span, :], packed_ref[pair, 0, span, :], 0, 0)
                for span in spans
            ]
            probs = []
            for one in scores:
                one = jnp.where(allowed, one, NEGATIVE)
                grown = jnp.exp((one - jnp.max(one, axis=0, keepdims=True)) * scale)
                one = grown * (1.0 / jnp.sum(grown, axis=0, keepdims=True))
                probs.append(one.astype(BF16))
            found = [dot(packed_ref[pair, 2, span, :], one) for span, one in zip(spans, probs)]
            for n, span in enumerate(spans):
                probs_ref[pair, first + n] = probs[n]
                context_ref[span, here] = found[n].astype(BF16)

    give(3, probs_ref, probs_hbm)
    give(4, context_ref, context_hbm)
    for pair in range(pairs):
        here = slice(pair * block, (pair + 1) * block)
        upright_ref[here, :] = context_ref[:, here].T
    load_out.wait()
    for at, size in tiles(model_width):
        rows_ref[:, at:at + size] += dot(upright_ref[...], w_out_ref[:, at:at + size])

    gain_sum_ref[...] = jnp.zeros_like(gain_sum_ref)
    load_cot.wait()

    @pl.loop(0, pairs)
    def _(pair):
        row_at = lax.broadcasted_iota(jnp.int32, (strip, 1), 0)
        alive = alive_of(row_at, live_ref[0, PAIR * pair], live_ref[0, PAIR * pair + 1], group)
        alive = jnp.where(alive, 1.0, 0.0)
        gain = gain_ref[...]
        out_rows = pl.ds(pl.multiple_of(pair * strip, strip), strip)
        for turn in range(JOIN):
            here = pl.ds(pl.multiple_of(pair * block + turn * strip, strip), strip)
            columns = slice(turn * model_width, (turn + 1) * model_width)
            attended = rows_ref[here, :]
            power = jnp.mean(attended * attended, axis=1, keepdims=True)
            inverse = lax.rsqrt(power + EPSILON)
            normalized = attended * inverse
            merged_ref[out_rows, columns] = (normalized * gain * alive).astype(BF16)
            grad_rows = cot_ref[out_rows, columns].astype(F32) * alive
            crossed = grad_rows * normalized
            gain_sum_ref[...] += jnp.sum(crossed.reshape(strip // 8, 8, model_width), axis=0)
            mean = jnp.mean(crossed * gain, axis=1, keepdims=True)
            d_att_ref[here, :] = (inverse * (grad_rows * gain - normalized * mean)).astype(BF16)

    give(5, merged_ref, merged_hbm)
    total = jnp.sum(gain_sum_ref[...], axis=0, keepdims=True)
    high = total.astype(BF16).astype(F32)
    at_row = lax.broadcasted_iota(jnp.int32, (LANES, model_width), 0)
    tail = jnp.where(at_row == 0, high, jnp.where(at_row == 1, total - high, 0.0))
    d_att_ref[row_count:, :] = tail.astype(BF16)

    for at, size in tiles(row_count + LANES, LANES):
        turned_ref[:, at:at + size] = d_att_ref[at:at + size, :].T
    by_core(turned_ref, att_keep_ref, att_send_ref)
    give(6, att_keep_ref, att_keep_hbm)
    give(7, att_send_ref, att_send_hbm)

    for at, size in tiles(inner):
        found = dot(w_out_ref[at:at + size, :], turned_ref[:, :row_count]).astype(BF16)
        for pair in range(pairs):
            d_context_ref[pair, at:at + size, :] = found[:, pair * block:(pair + 1) * block]
    give(8, d_context_ref, d_context_hbm)
    for n in sorted(outs):
        outs[n].wait()


def backward_kernel(*refs):
    for packed_ref, probs_ref, d_context_ref, d_packed_ref in zip(*[iter(refs)] * 4):
        _, heads, block, _ = probs_ref.shape
        height = d_context_ref.shape[1]
        head_width = height // heads
        scale = head_width ** (-0.5)
        spans = [slice(head * head_width, (head + 1) * head_width) for head in range(heads)]
        probs = [probs_ref[0, head] for head in range(heads)]
        d_probs = [
            dot(packed_ref[0, 2, 0, span, :], d_context_ref[0, span, :], 0, 0) for span in spans
        ]
        d_scores = []
        for low, one in zip(probs, d_probs):
            exact = low.astype(F32)
            inside = jnp.sum(one * exact, axis=0, keepdims=True)
            d_scores.append((exact * (one - inside) * scale).astype(BF16))
        founds = (
            [dot(packed_ref[0, 1, 0, span, :], one) for span, one in zip(spans, d_scores)],
            [dot(packed_ref[0, 0, 0, span, :], one, 1, 1) for span, one in zip(spans, d_scores)],
            [dot(d_context_ref[0, span, :], one, 1, 1) for span, one in zip(spans, probs)],
        )
        for n, found in enumerate(founds):
            for span, one in zip(spans, found):
                d_packed_ref[n * height + span.start:n * height + span.stop, :] = one.astype(BF16)


def product_kernel(*refs, taken, spans, extra_at):
    keep_ref, other_ref = refs[:2]
    rights = refs[2:-2]
    outs = refs[-2:]
    rank_rows, width = outs[0].shape[1:]
    depth = rights[0].shape[1]
    whole = rank_rows % 16 == 0
    lists = [[(n, g) for g in places] for n, places in enumerate(taken)]
    lists = [lists[0] + lists[1]] if whole else [[one] for one in lists[0] + lists[1]]
    count = len(rights) // 2
    sides = []
    for side in range(2):
        pieces = [
            ref[first:last] for ref, (first, last) in zip(rights[side * count:], spans)
        ]
        sides.append(jnp.concatenate(pieces, axis=0) if count > 1 else pieces[0])
    for ordered in lists:
        lefts = []
        for ref in (keep_ref, other_ref):
            pieces = [ref[g] for _, g in ordered]
            lefts.append(jnp.concatenate(pieces, axis=0) if whole else pieces[0])
        for at, size in tiles(sides[0].shape[0], 2 * TILE):
            total = dot(lefts[0][:, :depth], sides[0][at:at + size], 1, 1)
            total += dot(lefts[1][:, :depth], sides[1][at:at + size], 1, 1)
            place = [0, 0]
            for n, (side, g) in enumerate(ordered):
                spot = taken[side].index(g)
                outs[side][spot, :, at:at + size] = total[
                    n * rank_rows:(n + 1) * rank_rows
                ].astype(BF16)
        if extra_at is not None:
            column = lax.broadcasted_iota(jnp.int32, (LANES, LANES), 1)
            ones = jnp.where(column == extra_at % LANES, 1.0, 0.0).astype(BF16)
            total = dot(lefts[0][:, depth:], ones) + dot(lefts[1][:, depth:], ones)
            for n, (side, g) in enumerate(ordered):
                spot = taken[side].index(g)
                outs[side][spot, :, extra_at:] = total[
                    n * rank_rows:(n + 1) * rank_rows, extra_at % LANES:
                ].astype(BF16)


def product(left, own, theirs, spans, bit, extra_at=None):
    keep, other = left
    half, rank_rows, _ = keep.shape
    depth = own[0].shape[1]
    columns = sum(last - first for first, last in spans)
    width = columns if extra_at is None else ceil_to(columns + 1, LANES)
    sent = [g for g in range(half) if (g >> (bit - 1)) & 1]
    kept = [g for g in range(half) if g not in sent]
    shape = jax.ShapeDtypeStruct((half // 2, rank_rows, width), BF16)
    return pl.pallas_call(
        functools.partial(product_kernel, taken=(sent, kept), spans=spans, extra_at=extra_at),
        out_shape=[shape, shape],
        in_specs=[VMEM] * (2 + 2 * len(own)),
        out_specs=[VMEM] * 2,
        compiler_params=pltpu.CompilerParams(vmem_limit_bytes=20 * 2**20),
        cost_estimate=SMALL,
    )(keep, other, *own, *theirs)


def flip_pairs(size, bit):
    return [(i, i ^ (1 << bit)) for i in range(size)]


def pick(array, place, axis):
    return lax.dynamic_index_in_dim(array, place, axis, keepdims=False)


def add_low(first, second):
    return (first.astype(F32) + second.astype(F32)).astype(BF16)


class Sum:
    def __init__(self, kept, got, order):
        self.ranks, self.layers = lax.axis_size("dp"), lax.axis_size("vis")
        self.order = order[1:]
        self.left = [b for b in range(len(order), 0, -1) if b != order[0]]
        shape = (2,) * len(self.left) + kept.shape[1:]
        self.kept, self.got = kept.reshape(shape), [got.reshape(shape)]

    def after(self, other):
        *self.got, other = lax.optimization_barrier((*self.got, other))
        return other

    def step(self):
        got = self.got[0]
        if self.order:
            bit, *self.order = self.order
            axis = self.left.index(bit)
            halves = [
                [lax.index_in_dim(array, n, axis, keepdims=False) for n in range(2)]
                for array in (self.kept, got)
            ]
            sent = add_low(halves[0][1], halves[1][1])
            self.got = [lax.ppermute(sent, "dp", flip_pairs(self.ranks, bit))]
            self.kept = add_low(halves[0][0], halves[1][0])
            self.left.remove(bit)
            return
        self.kept, self.got = add_low(self.kept, got), []


class Spread:
    def __init__(self, wholes):
        layers, layer = lax.axis_size("vis"), lax.axis_index("vis")
        shards = [whole.reshape(layers, -1, whole.shape[-1]) for whole in wholes]

        def row_of(k):
            place = (layer + k) % layers
            return jnp.concatenate([pick(one, place, 0) for one in shards], axis=-1)

        self.kept = row_of(0)
        self.got = []
        for k in range(1, layers):
            pairs = [(i, (i + k) % layers) for i in range(layers)]
            self.got.append(lax.ppermute(row_of(k), "vis", pairs))

    def total(self):
        total = self.kept.astype(F32)
        for one in self.got:
            total = total + one.astype(F32)
        return total


VMEM = pl.BlockSpec(memory_space=pltpu.VMEM)
SMEM = pl.BlockSpec(memory_space=pltpu.SMEM)
ANY = pl.BlockSpec(memory_space=pl.ANY)


SMALL = pl.CostEstimate(flops=1, bytes_accessed=1, transcendentals=0)


def run_forward(rank, window_live, window_index, patches, gain, d_merged, w_qkv, w_out, half):
    row_count, model_width = patches.shape
    inner = w_out.shape[0]
    slots = window_live.shape[1]
    block = PAIR * row_count // slots
    pairs = slots // PAIR
    rank_rows = model_width // (2 * half)
    shapes = [
        d_merged.shape,
        (pairs, 3, inner, block),
        (pairs, HEADS, block, block),
        (pairs, inner, block),
        (inner, row_count),
        (half, rank_rows, row_count),
        (half, rank_rows, row_count),
        (half, rank_rows, row_count + LANES),
        (half, rank_rows, row_count + LANES),
    ]
    loads = 2 + len(tiles(3 * inner, inner // 2))
    return pl.pallas_call(
        forward_kernel,
        out_shape=[jax.ShapeDtypeStruct(s, BF16) for s in shapes],
        in_specs=[SMEM, SMEM, VMEM, VMEM, VMEM, ANY, ANY, ANY],
        out_specs=[ANY] * len(shapes),
        scratch_shapes=[pltpu.VMEM(a.shape, BF16) for a in (d_merged, w_qkv, w_out)]
        + [pltpu.VMEM(s, BF16) for s in shapes]
        + [
            pltpu.VMEM((row_count, model_width), F32),
            pltpu.VMEM((model_width, row_count), BF16),
            pltpu.VMEM((model_width, row_count + LANES), BF16),
            pltpu.VMEM((row_count, inner), BF16),
            pltpu.VMEM((row_count + LANES, model_width), BF16),
            pltpu.VMEM((8, model_width), F32),
            pltpu.VMEM((row_count, LANES), F32),
            pltpu.VMEM((row_count, row_count), BF16),
            pltpu.SemaphoreType.DMA((loads,)),
            pltpu.SemaphoreType.DMA((len(shapes),)),
        ],
        compiler_params=pltpu.CompilerParams(vmem_limit_bytes=58 * 2**20),
        cost_estimate=SMALL,
    )(rank, window_live, window_index, patches, gain, d_merged, w_qkv, w_out)


def run_backward(packed, probs, d_context, taken):
    pairs, _, inner, block = packed.shape
    heads, height = HEADS // PARTS, inner // PARTS

    def specs(part):
        return [
            pl.BlockSpec((1, 3, 1, height, block), lambda n: (n, 0, part, 0, 0)),
            pl.BlockSpec((1, heads, block, block), lambda n: (n, part, 0, 0)),
            pl.BlockSpec((1, height, block), lambda n: (n, part, 0)),
        ]

    def body(*refs):
        ins, outs = refs[:3 * len(taken)], refs[3 * len(taken):]
        backward_kernel(*[
            ref for n in range(len(taken)) for ref in (*ins[3 * n:3 * n + 3], outs[n])
        ])

    packed = packed.reshape(pairs, 3, PARTS, height, block)
    return pl.pallas_call(
        body,
        out_shape=[jax.ShapeDtypeStruct((3 * height, pairs * block), BF16) for _ in taken],
        grid=(pairs,),
        in_specs=[spec for part in taken for spec in specs(part)],
        out_specs=[pl.BlockSpec((3 * height, block), lambda n: (0, n)) for _ in taken],
        compiler_params=pltpu.CompilerParams(vmem_limit_bytes=56 * 2**20),
        cost_estimate=SMALL,
    )(*[packed, probs, d_context] * len(taken))


def on_device(patches, window_index, window_live, d_merged, w_qkv, w_out, merge_gain):
    model_width = patches.shape[1]
    inner = w_out.shape[0]
    ranks = lax.axis_size("dp")
    rank = lax.axis_index("dp")
    bits = ranks.bit_length() - 2
    after = lax.optimization_barrier
    (
        merged, packed, probs, d_context, context, norm_keep, norm_send, att_keep, att_send
    ) = run_forward(
        rank.reshape(1), window_live, window_index, patches,
        merge_gain.reshape(1, model_width), d_merged, w_qkv.T, w_out, ranks // 2,
    )

    def swap(array, bit=0):
        return lax.ppermute(array, "dp", flip_pairs(ranks, bit))

    along = list(range(1, bits + 1))
    by_x = along
    by_y = along[bits // 2:] + along[:bits // 2]
    height = inner // PARTS
    rest = 3 * height % LANES
    full = 3 * height - rest

    att_got, context_got, norm_got = swap(att_send), swap(context), swap(norm_send)
    (d_first,) = run_backward(packed, probs, d_context, (0,))
    first_got = swap(d_first)

    context_got, d_first = after((context_got, d_first))
    sent, kept_out = product(
        (att_keep, att_got), [context], [context_got], [(0, inner)], by_x[0], inner
    )
    sum_out = Sum(kept_out, swap(sent, by_x[0]), by_x)

    first_got, kept_out = after((first_got, kept_out))
    norm = (norm_keep, norm_got)
    sent, kept_1 = product(norm, [d_first], [first_got], [(0, full)], by_y[0])
    sum_1 = Sum(kept_1, swap(sent, by_y[0]), by_y)

    probs, kept_1 = after((probs, kept_1))
    d_second, d_third = run_backward(packed, probs, d_context, (1, 2))
    d_second = sum_out.after(d_second)
    second_got = swap(d_second)
    d_third = sum_1.after(d_third)
    third_got = swap(d_third)

    sum_out.step()
    sent, kept_2 = product(
        norm, [d_second, d_first], [second_got, first_got],
        [(0, 3 * height), (full, 3 * height)], by_x[0],
    )
    sum_2 = Sum(kept_2, swap(sent, by_x[0]), by_x)

    sum_1.step()
    third_got, kept_2 = after((third_got, kept_2))
    sent, kept_3 = product(norm, [d_third], [third_got], [(0, 3 * height)], by_y[0])
    kept_3 = sum_1.after(kept_3)
    kept_3 = sum_out.after(kept_3)
    sum_3 = Sum(kept_3, swap(sent, by_y[0]), by_y)

    for _ in range(bits - 2):
        for one in (sum_out, sum_1, sum_2, sum_3):
            one.step()
    sum_out.step()
    sum_1.step()
    early = Spread([sum_out.kept, sum_1.kept])
    early.kept = sum_2.after(early.kept)
    sum_2.step()
    early.kept = sum_3.after(early.kept)
    sum_3.step()
    total = early.total()
    total = sum_2.after(total)
    total = sum_3.after(total)
    sum_2.step()
    sum_3.step()
    width = sum_out.kept.shape[-1]
    total_out, total_1 = total[:, :width], total[:, width:]
    total = Spread([sum_2.kept, sum_3.kept]).total()
    width = sum_2.kept.shape[-1]
    total_2, total_3 = total[:, :width], total[:, width:]

    columns = []
    for part in range(3):
        at = part * height
        columns.append(total_1[:, at:min(at + height, full)])
        if part == 2 and rest:
            columns.append(total_2[:, 3 * height:])
        columns += [total_2[:, at:at + height], total_3[:, at:at + height]]
    total_qkv = jnp.concatenate(columns, axis=-1)
    return (merged, total_qkv, total_out[:, :inner].T, total_out[:, inner])


def solution(mesh):
    in_specs = (
        P(("dp", "vis"), None),
        P(("dp", "vis"), None),
        P(("dp", "vis"), None),
        P(("dp", "vis"), None),
        P(),
        P(),
        P(),
    )
    out_specs = (
        P(("dp", "vis"), None),
        P(("dp", "vis"), None),
        P(None, ("dp", "vis")),
        P(("dp", "vis")),
    )
    return jax.shard_map(
        on_device, mesh=mesh, in_specs=in_specs, out_specs=out_specs, check_vma=False
    )
```

```python
import functools

import jax
import jax.numpy as jnp
from jax import lax
from jax.experimental import pallas as pl
from jax.experimental.pallas import tpu as pltpu
from jax.sharding import PartitionSpec as P

HEADS = 12
STAGE = 4
JOIN = 4
PAIR = 2
LANES = 128
TILE = 256
EPSILON = 1e-06
NEGATIVE = -1e30
F32 = jnp.float32
BF16 = jnp.bfloat16


def ceil_to(size, step):
    return -(-size // step) * step


def dot(left, right, left_axis=1, right_axis=0):
    return lax.dot_general(
        left, right, (((left_axis,), (right_axis,)), ((), ())), preferred_element_type=F32
    )


def tiles(width, step=TILE):
    return [(at, min(step, width - at)) for at in range(0, width, step)]


def alive_of(place, live_first, live_second, group):
    limit = jnp.where((place // group) % PAIR == 0, live_first, live_second)
    return (place % group) * JOIN < limit


def forward_kernel(
    rank_ref, live_ref, index_ref, patches_ref, gain_ref, cot_hbm, w_qkv_hbm, w_out_hbm,
    merged_hbm, packed_hbm, probs_hbm, d_context_hbm, context_hbm,
    norm_keep_hbm, norm_send_hbm, att_keep_hbm, att_send_hbm,
    cot_ref, w_qkv_ref, w_out_ref,
    merged_ref, packed_ref, probs_ref, d_context_ref, context_ref,
    norm_keep_ref, norm_send_ref, att_keep_ref, att_send_ref,
    rows_ref, norm_ref, turned_ref, upright_ref, d_att_ref, gain_sum_ref, place_ref, chosen_ref,
    in_sems, out_sems,
):
    row_count, model_width = patches_ref.shape
    inner = w_out_ref.shape[0]
    head_width = inner // HEADS
    slots = live_ref.shape[1]
    win_rows = row_count // slots
    group = win_rows // JOIN
    block = PAIR * win_rows
    strip = PAIR * group
    pairs = slots // PAIR
    scale = head_width ** (-0.5)
    outs = {}

    parts = tiles(3 * inner, inner // 2)
    loads = [
        pltpu.make_async_copy(
            w_qkv_hbm.at[pl.ds(at, size)], w_qkv_ref.at[pl.ds(at, size)], in_sems.at[n]
        )
        for n, (at, size) in enumerate(parts)
    ]
    load_out = pltpu.make_async_copy(w_out_hbm, w_out_ref, in_sems.at[len(parts)])
    load_cot = pltpu.make_async_copy(cot_hbm, cot_ref, in_sems.at[len(parts) + 1])
    for load in loads + [load_out, load_cot]:
        load.start()

    def give(n, source, target):
        outs[n] = pltpu.make_async_copy(source, target, out_sems.at[n])
        outs[n].start()

    def by_core(source, keep, send):
        half, rank_rows, _ = keep.shape
        core, chip = rank_ref[0] & 1, rank_ref[0] >> 1
        for rank in range(2 * half):
            piece = source[rank * rank_rows:(rank + 1) * rank_rows, :]

            @pl.when(core == rank % 2)
            def _():
                keep[chip ^ (rank // 2)] = piece

            @pl.when(core != rank % 2)
            def _():
                send[chip ^ (rank // 2)] = piece

    places = jnp.broadcast_to(index_ref[...].astype(F32), (LANES, row_count))
    place_ref[...] = places.T
    raster = lax.broadcasted_iota(jnp.int32, (strip, row_count), 1)
    for pair in range(pairs):
        for turn in range(JOIN):
            at = pair * block + turn * strip
            place = place_ref[pl.ds(pair * block + turn, strip, stride=JOIN), :]
            found = raster == place[:, :1].astype(jnp.int32)
            chosen_ref[at:at + strip, :] = jnp.where(found, 1.0, 0.0).astype(BF16)
    for at, size in tiles(model_width):
        rows_ref[:, at:at + size] = dot(chosen_ref[...], patches_ref[:, at:at + size])

    for pair in range(pairs):
        here = slice(pair * block, (pair + 1) * block)
        rows = rows_ref[here, :]
        power = jnp.mean(rows * rows, axis=1, keepdims=True)
        normed = (rows * lax.rsqrt(power + EPSILON)).astype(BF16)
        norm_ref[:, here] = normed.T
    by_core(norm_ref, norm_keep_ref, norm_send_ref)
    give(0, norm_keep_ref, norm_keep_hbm)
    give(1, norm_send_ref, norm_send_hbm)

    for load, (first, height) in zip(loads, parts):
        load.wait()
        for at, size in tiles(height):
            at += first
            found = dot(w_qkv_ref[at:at + size, :], norm_ref[...]).astype(BF16)
            part, at = at // inner, at % inner
            for pair in range(pairs):
                packed_ref[pair, part, at:at + size, :] = found[:, pair * block:(pair + 1) * block]
    give(2, packed_ref, packed_hbm)

    @pl.loop(0, pairs)
    def _(pair):
        here = pl.ds(pl.multiple_of(pair * block, block), block)
        key_at = lax.broadcasted_iota(jnp.int32, (block, block), 0)
        query_at = lax.broadcasted_iota(jnp.int32, (block, block), 1)
        allowed = alive_of(key_at, live_ref[0, PAIR * pair], live_ref[0, PAIR * pair + 1], group)
        allowed = allowed & ((key_at // group) % PAIR == (query_at // group) % PAIR)
        for first in range(0, HEADS, STAGE):
            spans = [
                slice(head * head_width, (head + 1) * head_width)
                for head in range(first, first + STAGE)
            ]
            scores = [
                dot(packed_ref[pair, 1, span, :], packed_ref[pair, 0, span, :], 0, 0)
                for span in spans
            ]
            probs = []
            for one in scores:
                one = jnp.where(allowed, one, NEGATIVE)
                grown = jnp.exp((one - jnp.max(one, axis=0, keepdims=True)) * scale)
                one = grown * (1.0 / jnp.sum(grown, axis=0, keepdims=True))
                probs.append(one.astype(BF16))
            found = [dot(packed_ref[pair, 2, span, :], one) for span, one in zip(spans, probs)]
            for n, span in enumerate(spans):
                probs_ref[pair, first + n] = probs[n]
                context_ref[span, here] = found[n].astype(BF16)

    give(3, probs_ref, probs_hbm)
    give(4, context_ref, context_hbm)
    for pair in range(pairs):
        here = slice(pair * block, (pair + 1) * block)
        upright_ref[here, :] = context_ref[:, here].T
    load_out.wait()
    for at, size in tiles(model_width):
        rows_ref[:, at:at + size] += dot(upright_ref[...], w_out_ref[:, at:at + size])

    gain_sum_ref[...] = jnp.zeros_like(gain_sum_ref)
    load_cot.wait()

    @pl.loop(0, pairs)
    def _(pair):
        row_at = lax.broadcasted_iota(jnp.int32, (strip, 1), 0)
        alive = alive_of(row_at, live_ref[0, PAIR * pair], live_ref[0, PAIR * pair + 1], group)
        alive = jnp.where(alive, 1.0, 0.0)
        gain = gain_ref[...].reshape(1, model_width)
        out_rows = pl.ds(pl.multiple_of(pair * strip, strip), strip)
        for turn in range(JOIN):
            here = pl.ds(pl.multiple_of(pair * block + turn * strip, strip), strip)
            columns = slice(turn * model_width, (turn + 1) * model_width)
            attended = rows_ref[here, :]
            power = jnp.mean(attended * attended, axis=1, keepdims=True)
            inverse = lax.rsqrt(power + EPSILON)
            normalized = attended * inverse
            merged_ref[out_rows, columns] = (normalized * gain * alive).astype(BF16)
            grad_rows = cot_ref[out_rows, columns].astype(F32) * alive
            crossed = grad_rows * normalized
            gain_sum_ref[...] += jnp.sum(crossed.reshape(strip // 8, 8, model_width), axis=0)
            mean = jnp.mean(crossed * gain, axis=1, keepdims=True)
            d_att_ref[here, :] = (inverse * (grad_rows * gain - normalized * mean)).astype(BF16)

    give(5, merged_ref, merged_hbm)
    total = jnp.sum(gain_sum_ref[...], axis=0, keepdims=True)
    high = total.astype(BF16).astype(F32)
    at_row = lax.broadcasted_iota(jnp.int32, (LANES, model_width), 0)
    tail = jnp.where(at_row == 0, high, jnp.where(at_row == 1, total - high, 0.0))
    d_att_ref[row_count:, :] = tail.astype(BF16)

    for at, size in tiles(row_count + LANES, LANES):
        turned_ref[:, at:at + size] = d_att_ref[at:at + size, :].T
    by_core(turned_ref, att_keep_ref, att_send_ref)
    give(6, att_keep_ref, att_keep_hbm)
    give(7, att_send_ref, att_send_hbm)

    for at, size in tiles(inner):
        found = dot(w_out_ref[at:at + size, :], turned_ref[:, :row_count]).astype(BF16)
        for pair in range(pairs):
            d_context_ref[pair, at:at + size, :] = found[:, pair * block:(pair + 1) * block]
    give(8, d_context_ref, d_context_hbm)
    for n in sorted(outs):
        outs[n].wait()


def backward_kernel(packed_ref, probs_ref, d_context_ref, *outs):
    _, heads, block, _ = probs_ref.shape
    inner = d_context_ref.shape[1]
    head_width = inner // heads
    scale = head_width ** (-0.5)

    def put(at, value):
        value = value.astype(BF16)
        for ref in outs:
            taken = max(0, min(ref.shape[0] - at, value.shape[0]))
            if taken > 0:
                ref[at:at + taken, :] = value[:taken]
                value = value[taken:]
                at += taken
            at -= ref.shape[0]

    for first in range(0, heads, STAGE):
        together = range(first, first + STAGE)
        spans = [slice(head * head_width, (head + 1) * head_width) for head in together]
        probs = [probs_ref[0, head] for head in together]
        d_probs = [
            dot(packed_ref[0, 2, span, :], d_context_ref[0, span, :], 0, 0) for span in spans
        ]
        d_scores = []
        for low, one in zip(probs, d_probs):
            exact = low.astype(F32)
            inside = jnp.sum(one * exact, axis=0, keepdims=True)
            d_scores.append((exact * (one - inside) * scale).astype(BF16))
        founds = (
            [dot(packed_ref[0, 1, span, :], one) for span, one in zip(spans, d_scores)],
            [dot(packed_ref[0, 0, span, :], one, 1, 1) for span, one in zip(spans, d_scores)],
            [dot(d_context_ref[0, span, :], one, 1, 1) for span, one in zip(spans, probs)],
        )
        for n, found in enumerate(founds):
            for span, one in zip(spans, found):
                put(n * inner + span.start, one)


def product_kernel(keep_ref, other_ref, right_ref, right_other_ref, *outs, pieces, extra_at):
    half, rank_rows, _ = keep_ref.shape
    depth = right_ref.shape[1]
    whole = rank_rows % 16 == 0
    for groups in [list(range(half))] if whole else [[g] for g in range(half)]:
        lefts = []
        for ref in (keep_ref, other_ref):
            rows = [ref[g] for g in groups]
            lefts.append(jnp.concatenate(rows, axis=0) if whole else rows[0])
        number = 0
        for (first, last), lists in pieces:
            def put(total, at):
                for n, g in enumerate(groups):
                    for ref, held in zip(outs[number:], lists):
                        if g in held:
                            ref[held.index(g), :, at:at + total.shape[1]] = total[
                                n * rank_rows:(n + 1) * rank_rows
                            ].astype(BF16)

            for at, size in tiles(last - first, 2 * TILE):
                span = slice(first + at, first + at + size)
                total = dot(lefts[0][:, :depth], right_ref[span, :], 1, 1)
                total += dot(lefts[1][:, :depth], right_other_ref[span, :], 1, 1)
                put(total, at)
            if extra_at is not None:
                column = lax.broadcasted_iota(jnp.int32, (LANES, LANES), 1)
                ones = jnp.where(column == extra_at % LANES, 1.0, 0.0).astype(BF16)
                total = dot(lefts[0][:, depth:], ones) + dot(lefts[1][:, depth:], ones)
                put(total[:, extra_at % LANES:], extra_at)
            number += len(lists)


def product(left, right, pieces, extra_at=None):
    keep, other = left
    half, rank_rows, _ = keep.shape
    taken, shapes, counts = [], [], []
    for (first, last), axis in pieces:
        sent = [] if axis == "vis" else [g for g in range(half) if (g >> (axis - 1)) & 1]
        lists = [held for held in (sent, [g for g in range(half) if g not in sent]) if held]
        width = last - first if extra_at is None else ceil_to(last - first + 1, LANES)
        taken.append(((first, last), lists))
        shapes += [jax.ShapeDtypeStruct((len(held), rank_rows, width), BF16) for held in lists]
        counts.append(len(lists))
    found = pl.pallas_call(
        functools.partial(product_kernel, pieces=taken, extra_at=extra_at),
        out_shape=shapes,
        in_specs=[VMEM] * 4,
        out_specs=[VMEM] * len(shapes),
        compiler_params=pltpu.CompilerParams(vmem_limit_bytes=24 * 2**20),
        cost_estimate=SMALL,
    )(keep, other, *right)
    return [found[sum(counts[:n]):sum(counts[:n + 1])] for n in range(len(counts))]


def flip_pairs(size, bit):
    return [(i, i ^ (1 << bit)) for i in range(size)]


def pick(array, place, axis):
    return lax.dynamic_index_in_dim(array, place, axis, keepdims=False)


def together(arrays, others):
    found = lax.optimization_barrier((*arrays, *others))
    return list(found[:len(arrays)]), list(found[len(arrays):])


class Sum:
    def __init__(self, kept, order):
        self.ranks = lax.axis_size("dp")
        self.order = list(order)
        self.left = [b for b in range(self.ranks.bit_length() - 2, 0, -1)]
        self.kept, self.got = kept, []

    def first(self, sent, kept):
        self.arrived(lax.ppermute(sent, "dp", flip_pairs(self.ranks, self.order[0])), kept)

    def arrived(self, got, kept):
        bit, *self.order = self.order
        self.left.remove(bit)
        shape = (2,) * len(self.left) + kept.shape[1:]
        self.kept, self.got = kept.reshape(shape), [got.reshape(shape)]

    def after(self, others):
        self.got, others = together(self.got, others)
        return others

    def step(self):
        axis, *self.order = self.order
        terms = [self.kept, *self.got]
        if axis == "vis":
            layers, layer = lax.axis_size("vis"), lax.axis_index("vis")
            whole = total_of(terms).astype(BF16)
            places = 2 ** len(self.left)
            shards = whole.reshape(places, layers, -1, whole.shape[-1])
            self.kept = pick(shards, layer, 1)
            self.got = []
            for k in range(1, layers):
                pairs = [(i, (i + k) % layers) for i in range(layers)]
                sent = pick(shards, (layer + k) % layers, 1)
                self.got.append(lax.ppermute(sent, "vis", pairs))
            return
        sent = self.part(axis)
        self.got = [lax.ppermute(sent, "dp", flip_pairs(self.ranks, axis))]

    def part(self, axis):
        shape = (2,) * len(self.left) + self.kept.shape[-2:]
        at = self.left.index(axis)
        terms = [one.reshape(shape) for one in (self.kept, *self.got)]
        self.kept, sent = [
            total_of([lax.index_in_dim(one, n, at, keepdims=False) for one in terms]).astype(BF16)
            for n in range(2)
        ]
        self.left.remove(axis)
        return sent

    def total(self):
        return total_of([self.kept, *self.got])

    def whole(self):
        return self.total().astype(BF16).reshape(self.kept.shape[-2:])


def total_of(terms):
    total = terms[0].astype(F32)
    for one in terms[1:]:
        total = total + one.astype(F32)
    return total


class Spread(Sum):
    def __init__(self, wholes):
        layers, layer = lax.axis_size("vis"), lax.axis_index("vis")
        shards = [whole.reshape(layers, -1, whole.shape[-1]) for whole in wholes]

        def row_of(k):
            place = (layer + k) % layers
            return jnp.concatenate([pick(one, place, 0) for one in shards], axis=-1)

        self.kept = row_of(0)
        self.got = []
        for k in range(1, layers):
            pairs = [(i, (i + k) % layers) for i in range(layers)]
            self.got.append(lax.ppermute(row_of(k), "vis", pairs))


VMEM = pl.BlockSpec(memory_space=pltpu.VMEM)
SMEM = pl.BlockSpec(memory_space=pltpu.SMEM)
ANY = pl.BlockSpec(memory_space=pl.ANY)


SMALL = pl.CostEstimate(flops=1, bytes_accessed=1, transcendentals=0)


def run_forward(rank, window_live, window_index, patches, gain, d_merged, w_qkv, w_out, half):
    row_count, model_width = patches.shape
    inner = w_out.shape[0]
    slots = window_live.shape[1]
    block = PAIR * row_count // slots
    pairs = slots // PAIR
    rank_rows = model_width // (2 * half)
    shapes = [
        d_merged.shape,
        (pairs, 3, inner, block),
        (pairs, HEADS, block, block),
        (pairs, inner, block),
        (inner, row_count),
        (half, rank_rows, row_count),
        (half, rank_rows, row_count),
        (half, rank_rows, row_count + LANES),
        (half, rank_rows, row_count + LANES),
    ]
    loads = 2 + len(tiles(3 * inner, inner // 2))
    return pl.pallas_call(
        forward_kernel,
        out_shape=[jax.ShapeDtypeStruct(s, BF16) for s in shapes],
        in_specs=[SMEM, SMEM, VMEM, VMEM, VMEM, ANY, ANY, ANY],
        out_specs=[ANY] * len(shapes),
        scratch_shapes=[pltpu.VMEM(a.shape, BF16) for a in (d_merged, w_qkv, w_out)]
        + [pltpu.VMEM(s, BF16) for s in shapes]
        + [
            pltpu.VMEM((row_count, model_width), F32),
            pltpu.VMEM((model_width, row_count), BF16),
            pltpu.VMEM((model_width, row_count + LANES), BF16),
            pltpu.VMEM((row_count, inner), BF16),
            pltpu.VMEM((row_count + LANES, model_width), BF16),
            pltpu.VMEM((8, model_width), F32),
            pltpu.VMEM((row_count, LANES), F32),
            pltpu.VMEM((row_count, row_count), BF16),
            pltpu.SemaphoreType.DMA((loads,)),
            pltpu.SemaphoreType.DMA((len(shapes),)),
        ],
        compiler_params=pltpu.CompilerParams(vmem_limit_bytes=58 * 2**20),
        cost_estimate=SMALL,
    )(rank, window_live, window_index, patches, gain, d_merged, w_qkv, w_out)


def run_backward(packed, probs, d_context, heights):
    pairs, _, inner, block = packed.shape
    return pl.pallas_call(
        backward_kernel,
        out_shape=[jax.ShapeDtypeStruct((h, pairs * block), BF16) for h in heights],
        grid=(pairs,),
        in_specs=[
            pl.BlockSpec((1, 3, inner, block), lambda n: (n, 0, 0, 0)),
            pl.BlockSpec((1, HEADS, block, block), lambda n: (n, 0, 0, 0)),
            pl.BlockSpec((1, inner, block), lambda n: (n, 0, 0)),
        ],
        out_specs=[pl.BlockSpec((h, block), lambda n: (0, n)) for h in heights],
        compiler_params=pltpu.CompilerParams(vmem_limit_bytes=56 * 2**20),
        cost_estimate=SMALL,
    )(packed, probs, d_context)


def on_device(patches, window_index, window_live, d_merged, w_qkv, w_out, merge_gain):
    model_width = patches.shape[1]
    inner = w_out.shape[0]
    ranks = lax.axis_size("dp")
    rank = lax.axis_index("dp")
    bits = ranks.bit_length() - 2
    (
        merged, packed, probs, d_context, context, norm_keep, norm_send, att_keep, att_send
    ) = run_forward(
        rank.reshape(1), window_live, window_index, patches,
        merge_gain, d_merged, w_qkv.T, w_out, ranks // 2,
    )

    def swap(array):
        return lax.ppermute(array, "dp", flip_pairs(ranks, 0))

    along = list(range(1, bits + 1))
    by_x = along + ["vis"]
    by_y = along[bits // 2:] + along[:bits // 2] + ["vis"]
    early, late, last = 8 * LANES, 15 * LANES, 3 * inner

    got = [swap(context), swap(att_send), swap(norm_send)]
    d_first, d_last = run_backward(packed, probs, d_context, (early, last - early))
    got, (d_first, d_last) = together(got, [d_first, d_last])
    context_got, att_got, norm_got = got
    first_got = swap(d_first)
    norm = (norm_keep, norm_got)

    ((sent, kept),) = product(
        (att_keep, att_got), (context, context_got), [((0, inner), by_x[0])], inner
    )
    sum_out = Sum(None, by_x)
    sum_out.first(sent, kept)

    (first_got,), (d_last, sum_out.kept) = together([first_got], [d_last, sum_out.kept])
    last_got = swap(d_last)
    ((sent, kept),) = product(norm, (d_first, first_got), [((0, early), by_y[0])])
    sum_1 = Sum(None, by_y)
    sum_1.first(sent, kept)

    (last_got,), (sum_1.kept,) = together([last_got], [sum_1.kept])
    (sent_2, kept_2), (sent_3, kept_3) = product(
        norm, (d_last, last_got), [((0, late - early), by_x[0]), ((late - early, last - early), by_y[0])]
    )

    kept_2, sent_2 = sum_out.after([kept_2, sent_2])
    kept_3, sent_3 = sum_1.after([kept_3, sent_3])
    sum_2, sum_3 = Sum(None, by_x), Sum(None, by_y)
    sum_2.first(sent_2, kept_2)
    sum_3.first(sent_3, kept_3)
    for _ in range(bits - 1):
        sum_out.step()
        sum_1.step()
    spread_1 = Spread([sum_out.whole(), sum_1.whole()])
    for _ in range(bits - 1):
        sum_2.step()
        sum_3.step()
    wholes = [sum_2.whole(), sum_3.whole()]
    spread_1.got, wholes = together(spread_1.got, wholes)
    spread_2 = Spread(wholes)
    total, total_late = spread_1.total(), spread_2.total()
    width = ceil_to(inner + 1, LANES)
    total_out, total_1 = total[:, :width], total[:, width:]
    total_qkv = jnp.concatenate([total_1, total_late], axis=-1)
    return (merged, total_qkv, total_out[:, :inner].T, total_out[:, inner])


def solution(mesh):
    in_specs = (
        P(("dp", "vis"), None),
        P(("dp", "vis"), None),
        P(("dp", "vis"), None),
        P(("dp", "vis"), None),
        P(),
        P(),
        P(),
    )
    out_specs = (
        P(("dp", "vis"), None),
        P(("dp", "vis"), None),
        P(None, ("dp", "vis")),
        P(("dp", "vis")),
    )
    return jax.shard_map(
        on_device, mesh=mesh, in_specs=in_specs, out_specs=out_specs, check_vma=False
    )
```

```python
import functools

import jax
import jax.numpy as jnp
from jax import lax
from jax.experimental import pallas as pl
from jax.experimental.pallas import tpu as pltpu
from jax.sharding import PartitionSpec as P

HEADS = 12
STAGE = 12
JOIN = 4
PAIR = 2
LANES = 128
TILE = 256
EPSILON = 1e-06
NEGATIVE = -1e30
F32 = jnp.float32
BF16 = jnp.bfloat16


def ceil_to(size, step):
    return -(-size // step) * step


def dot(left, right, left_axis=1, right_axis=0):
    return lax.dot_general(
        left, right, (((left_axis,), (right_axis,)), ((), ())), preferred_element_type=F32
    )


def tiles(width, step=TILE):
    return [(at, min(step, width - at)) for at in range(0, width, step)]


def alive_of(place, live_first, live_second, group):
    limit = jnp.where((place // group) % PAIR == 0, live_first, live_second)
    return (place % group) * JOIN < limit


def forward_kernel(
    rank_ref, live_ref, index_ref, patches_ref, gain_ref, cot_hbm, w_qkv_hbm, w_out_hbm,
    merged_hbm, packed_hbm, probs_hbm, d_context_hbm, context_hbm,
    norm_keep_hbm, norm_send_hbm, att_keep_hbm, att_send_hbm,
    cot_ref, w_qkv_ref, w_out_ref,
    merged_ref, packed_ref, probs_ref, d_context_ref, context_ref,
    norm_keep_ref, norm_send_ref, att_keep_ref, att_send_ref,
    rows_ref, norm_ref, turned_ref, upright_ref, d_att_ref, gain_sum_ref, place_ref, chosen_ref,
    in_sems, out_sems,
):
    row_count, model_width = patches_ref.shape
    inner = w_out_ref.shape[0]
    head_width = inner // HEADS
    slots = live_ref.shape[1]
    win_rows = row_count // slots
    group = win_rows // JOIN
    block = PAIR * win_rows
    strip = PAIR * group
    pairs = slots // PAIR
    scale = head_width ** (-0.5)
    outs = {}

    parts = tiles(3 * inner, inner // 2)
    loads = [
        pltpu.make_async_copy(
            w_qkv_hbm.at[pl.ds(at, size)], w_qkv_ref.at[pl.ds(at, size)], in_sems.at[n]
        )
        for n, (at, size) in enumerate(parts)
    ]
    load_out = pltpu.make_async_copy(w_out_hbm, w_out_ref, in_sems.at[len(parts)])
    load_cot = pltpu.make_async_copy(cot_hbm, cot_ref, in_sems.at[len(parts) + 1])
    for load in loads + [load_out, load_cot]:
        load.start()

    def give(n, source, target):
        outs[n] = pltpu.make_async_copy(source, target, out_sems.at[n])
        outs[n].start()

    def by_core(source, keep, send):
        half, rank_rows, _ = keep.shape
        core, chip = rank_ref[0] & 1, rank_ref[0] >> 1
        for rank in range(2 * half):
            piece = source[rank * rank_rows:(rank + 1) * rank_rows, :]

            @pl.when(core == rank % 2)
            def _():
                keep[chip ^ (rank // 2)] = piece

            @pl.when(core != rank % 2)
            def _():
                send[chip ^ (rank // 2)] = piece

    places = jnp.broadcast_to(index_ref[...].astype(F32), (LANES, row_count))
    place_ref[...] = places.T
    raster = lax.broadcasted_iota(jnp.int32, (strip, row_count), 1)
    for pair in range(pairs):
        for turn in range(JOIN):
            at = pair * block + turn * strip
            place = place_ref[pl.ds(pair * block + turn, strip, stride=JOIN), :]
            found = raster == place[:, :1].astype(jnp.int32)
            chosen_ref[at:at + strip, :] = jnp.where(found, 1.0, 0.0).astype(BF16)
    for at, size in tiles(model_width):
        rows_ref[:, at:at + size] = dot(chosen_ref[...], patches_ref[:, at:at + size])

    @pl.loop(0, row_count // strip)
    def _(n):
        here = pl.ds(pl.multiple_of(n * strip, strip), strip)
        rows = rows_ref[here, :]
        power = jnp.mean(rows * rows, axis=1, keepdims=True)
        d_att_ref[here, :] = (rows * lax.rsqrt(power + EPSILON)).astype(BF16)

    for pair in range(pairs):
        here = slice(pair * block, (pair + 1) * block)
        norm_ref[:, here] = d_att_ref[here, :].T
    by_core(norm_ref, norm_keep_ref, norm_send_ref)
    give(0, norm_keep_ref, norm_keep_hbm)
    give(1, norm_send_ref, norm_send_hbm)

    for load, (first, height) in zip(loads, parts):
        load.wait()
        for at, size in tiles(height):
            at += first
            found = dot(w_qkv_ref[at:at + size, :], norm_ref[...]).astype(BF16)
            part, at = at // inner, at % inner
            for pair in range(pairs):
                packed_ref[pair, part, at:at + size, :] = found[:, pair * block:(pair + 1) * block]
    give(2, packed_ref, packed_hbm)

    @pl.loop(0, pairs)
    def _(pair):
        here = pl.ds(pl.multiple_of(pair * block, block), block)
        key_at = lax.broadcasted_iota(jnp.int32, (block, block), 0)
        query_at = lax.broadcasted_iota(jnp.int32, (block, block), 1)
        allowed = alive_of(key_at, live_ref[0, PAIR * pair], live_ref[0, PAIR * pair + 1], group)
        allowed = allowed & ((key_at // group) % PAIR == (query_at // group) % PAIR)
        for first in range(0, HEADS, STAGE):
            spans = [
                slice(head * head_width, (head + 1) * head_width)
                for head in range(first, first + STAGE)
            ]
            scores = [
                dot(packed_ref[pair, 1, span, :], packed_ref[pair, 0, span, :], 0, 0)
                for span in spans
            ]
            probs = []
            for one in scores:
                one = jnp.where(allowed, one, NEGATIVE)
                grown = jnp.exp((one - jnp.max(one, axis=0, keepdims=True)) * scale)
                one = grown * (1.0 / jnp.sum(grown, axis=0, keepdims=True))
                probs.append(one.astype(BF16))
            found = [dot(packed_ref[pair, 2, span, :], one) for span, one in zip(spans, probs)]
            for n, span in enumerate(spans):
                probs_ref[pair, first + n] = probs[n]
                context_ref[span, here] = found[n].astype(BF16)

    give(3, probs_ref, probs_hbm)
    give(4, context_ref, context_hbm)
    for pair in range(pairs):
        here = slice(pair * block, (pair + 1) * block)
        upright_ref[here, :] = context_ref[:, here].T
    load_out.wait()
    for at, size in tiles(model_width):
        rows_ref[:, at:at + size] += dot(upright_ref[...], w_out_ref[:, at:at + size])

    gain_sum_ref[...] = jnp.zeros_like(gain_sum_ref)
    load_cot.wait()

    @pl.loop(0, pairs * PAIR)
    def _(window):
        pair, second = window // PAIR, window % PAIR
        row_at = lax.broadcasted_iota(jnp.int32, (group, 1), 0)
        alive = jnp.where(row_at * JOIN < live_ref[0, window], 1.0, 0.0)
        gain = gain_ref[...].reshape(1, model_width)
        out_rows = pl.ds(pl.multiple_of(window * group, group), group)
        for turn in range(JOIN):
            start = pair * block + turn * strip + second * group
            here = pl.ds(pl.multiple_of(start, group), group)
            columns = slice(turn * model_width, (turn + 1) * model_width)
            attended = rows_ref[here, :]
            power = jnp.mean(attended * attended, axis=1, keepdims=True)
            inverse = lax.rsqrt(power + EPSILON)
            normalized = attended * inverse
            merged_ref[out_rows, columns] = (normalized * gain * alive).astype(BF16)
            grad_rows = cot_ref[out_rows, columns].astype(F32) * alive
            crossed = grad_rows * normalized
            gain_sum_ref[...] += jnp.sum(crossed.reshape(group // 8, 8, model_width), axis=0)
            mean = jnp.mean(crossed * gain, axis=1, keepdims=True)
            d_att_ref[here, :] = (inverse * (grad_rows * gain - normalized * mean)).astype(BF16)

    give(5, merged_ref, merged_hbm)
    total = jnp.sum(gain_sum_ref[...], axis=0, keepdims=True)
    high = total.astype(BF16).astype(F32)
    at_row = lax.broadcasted_iota(jnp.int32, (LANES, model_width), 0)
    tail = jnp.where(at_row == 0, high, jnp.where(at_row == 1, total - high, 0.0))
    d_att_ref[row_count:, :] = tail.astype(BF16)

    for at, size in tiles(row_count + LANES, LANES):
        turned_ref[:, at:at + size] = d_att_ref[at:at + size, :].T
    by_core(turned_ref, att_keep_ref, att_send_ref)
    give(6, att_keep_ref, att_keep_hbm)
    give(7, att_send_ref, att_send_hbm)

    for at, size in tiles(inner):
        found = dot(w_out_ref[at:at + size, :], turned_ref[:, :row_count]).astype(BF16)
        for pair in range(pairs):
            d_context_ref[pair, at:at + size, :] = found[:, pair * block:(pair + 1) * block]
    give(8, d_context_ref, d_context_hbm)
    for n in sorted(outs):
        outs[n].wait()


def backward_kernel(packed_ref, probs_ref, d_context_ref, *outs):
    _, heads, block, _ = probs_ref.shape
    inner = d_context_ref.shape[1]
    head_width = inner // heads
    scale = head_width ** (-0.5)

    def put(at, value):
        value = value.astype(BF16)
        for ref in outs:
            taken = max(0, min(ref.shape[0] - at, value.shape[0]))
            if taken > 0:
                ref[at:at + taken, :] = value[:taken]
                value = value[taken:]
                at += taken
            at -= ref.shape[0]

    for first in range(0, heads, STAGE):
        together = range(first, first + STAGE)
        spans = [slice(head * head_width, (head + 1) * head_width) for head in together]
        probs = [probs_ref[0, head] for head in together]
        d_probs = [
            dot(packed_ref[0, 2, span, :], d_context_ref[0, span, :], 0, 0) for span in spans
        ]
        d_scores = []
        for low, one in zip(probs, d_probs):
            exact = low.astype(F32)
            inside = jnp.sum(one * exact, axis=0, keepdims=True)
            d_scores.append((exact * (one - inside) * scale).astype(BF16))
        founds = (
            [dot(packed_ref[0, 1, span, :], one) for span, one in zip(spans, d_scores)],
            [dot(packed_ref[0, 0, span, :], one, 1, 1) for span, one in zip(spans, d_scores)],
            [dot(d_context_ref[0, span, :], one, 1, 1) for span, one in zip(spans, probs)],
        )
        for n, found in enumerate(founds):
            for span, one in zip(spans, found):
                put(n * inner + span.start, one)


def product_kernel(keep_ref, other_ref, right_ref, right_other_ref, *outs, pieces, extra_at):
    half, rank_rows, _ = keep_ref.shape
    depth = right_ref.shape[1]
    whole = rank_rows % 16 == 0
    for groups in [list(range(half))] if whole else [[g] for g in range(half)]:
        lefts = []
        for ref in (keep_ref, other_ref):
            rows = [ref[g] for g in groups]
            lefts.append(jnp.concatenate(rows, axis=0) if whole else rows[0])
        number = 0
        for (first, last), lists in pieces:
            def put(total, at):
                for n, g in enumerate(groups):
                    for ref, held in zip(outs[number:], lists):
                        if g in held:
                            ref[held.index(g), :, at:at + total.shape[1]] = total[
                                n * rank_rows:(n + 1) * rank_rows
                            ].astype(BF16)

            for at, size in tiles(last - first, 2 * TILE):
                span = slice(first + at, first + at + size)
                total = dot(lefts[0][:, :depth], right_ref[span, :], 1, 1)
                total += dot(lefts[1][:, :depth], right_other_ref[span, :], 1, 1)
                put(total, at)
            if extra_at is not None:
                column = lax.broadcasted_iota(jnp.int32, (LANES, LANES), 1)
                ones = jnp.where(column == extra_at % LANES, 1.0, 0.0).astype(BF16)
                total = dot(lefts[0][:, depth:], ones) + dot(lefts[1][:, depth:], ones)
                put(total[:, extra_at % LANES:], extra_at)
            number += len(lists)


def product(left, right, pieces, extra_at=None):
    keep, other = left
    half, rank_rows, _ = keep.shape
    taken, shapes, counts = [], [], []
    for (first, last), axis in pieces:
        sent = [] if axis == "vis" else [g for g in range(half) if (g >> (axis - 1)) & 1]
        lists = [held for held in (sent, [g for g in range(half) if g not in sent]) if held]
        width = last - first if extra_at is None else ceil_to(last - first + 1, LANES)
        taken.append(((first, last), lists))
        shapes += [jax.ShapeDtypeStruct((len(held), rank_rows, width), BF16) for held in lists]
        counts.append(len(lists))
    found = pl.pallas_call(
        functools.partial(product_kernel, pieces=taken, extra_at=extra_at),
        out_shape=shapes,
        in_specs=[VMEM] * 4,
        out_specs=[VMEM] * len(shapes),
        compiler_params=pltpu.CompilerParams(vmem_limit_bytes=14 * 2**20),
        cost_estimate=SMALL,
    )(keep, other, *right)
    return [found[sum(counts[:n]):sum(counts[:n + 1])] for n in range(len(counts))]


def flip_pairs(size, bit):
    return [(i, i ^ (1 << bit)) for i in range(size)]


def pick(array, place, axis):
    return lax.dynamic_index_in_dim(array, place, axis, keepdims=False)


def together(arrays, others):
    found = lax.optimization_barrier((*arrays, *others))
    return list(found[:len(arrays)]), list(found[len(arrays):])


class Sum:
    def __init__(self, kept, order):
        self.ranks = lax.axis_size("dp")
        self.order = list(order)
        self.left = [b for b in range(self.ranks.bit_length() - 2, 0, -1)]
        self.kept, self.got = kept, []

    def first(self, sent, kept):
        self.arrived(lax.ppermute(sent, "dp", flip_pairs(self.ranks, self.order[0])), kept)

    def arrived(self, got, kept):
        bit, *self.order = self.order
        self.left.remove(bit)
        shape = (2,) * len(self.left) + kept.shape[1:]
        self.kept, self.got = kept.reshape(shape), [got.reshape(shape)]

    def after(self, others):
        self.got, others = together(self.got, others)
        return others

    def step(self):
        axis, *self.order = self.order
        terms = [self.kept, *self.got]
        if axis == "vis":
            layers, layer = lax.axis_size("vis"), lax.axis_index("vis")
            whole = total_of(terms).astype(BF16)
            places = 2 ** len(self.left)
            shards = whole.reshape(places, layers, -1, whole.shape[-1])
            self.kept = pick(shards, layer, 1)
            self.got = []
            for k in range(1, layers):
                pairs = [(i, (i + k) % layers) for i in range(layers)]
                sent = pick(shards, (layer + k) % layers, 1)
                self.got.append(lax.ppermute(sent, "vis", pairs))
            return
        sent = self.part(axis)
        self.got = [lax.ppermute(sent, "dp", flip_pairs(self.ranks, axis))]

    def part(self, axis):
        shape = (2,) * len(self.left) + self.kept.shape[-2:]
        at = self.left.index(axis)
        terms = [one.reshape(shape) for one in (self.kept, *self.got)]
        self.kept, sent = [
            total_of([lax.index_in_dim(one, n, at, keepdims=False) for one in terms]).astype(BF16)
            for n in range(2)
        ]
        self.left.remove(axis)
        return sent

    def total(self):
        return total_of([self.kept, *self.got])

    def whole(self):
        return self.total().astype(BF16).reshape(self.kept.shape[-2:])


def total_of(terms):
    total = terms[0].astype(F32)
    for one in terms[1:]:
        total = total + one.astype(F32)
    return total


class Spread(Sum):
    def __init__(self, wholes):
        layers, layer = lax.axis_size("vis"), lax.axis_index("vis")
        shards = [whole.reshape(layers, -1, whole.shape[-1]) for whole in wholes]

        def row_of(k):
            place = (layer + k) % layers
            return jnp.concatenate([pick(one, place, 0) for one in shards], axis=-1)

        self.kept = row_of(0)
        self.got = []
        for k in range(1, layers):
            pairs = [(i, (i + k) % layers) for i in range(layers)]
            self.got.append(lax.ppermute(row_of(k), "vis", pairs))


VMEM = pl.BlockSpec(memory_space=pltpu.VMEM)
SMEM = pl.BlockSpec(memory_space=pltpu.SMEM)
ANY = pl.BlockSpec(memory_space=pl.ANY)


SMALL = pl.CostEstimate(flops=1, bytes_accessed=1, transcendentals=0)


def run_forward(rank, window_live, window_index, patches, gain, d_merged, w_qkv, w_out, half):
    row_count, model_width = patches.shape
    inner = w_out.shape[0]
    slots = window_live.shape[1]
    block = PAIR * row_count // slots
    pairs = slots // PAIR
    rank_rows = model_width // (2 * half)
    shapes = [
        d_merged.shape,
        (pairs, 3, inner, block),
        (pairs, HEADS, block, block),
        (pairs, inner, block),
        (inner, row_count),
        (half, rank_rows, row_count),
        (half, rank_rows, row_count),
        (half, rank_rows, row_count + LANES),
        (half, rank_rows, row_count + LANES),
    ]
    loads = 2 + len(tiles(3 * inner, inner // 2))
    return pl.pallas_call(
        forward_kernel,
        out_shape=[jax.ShapeDtypeStruct(s, BF16) for s in shapes],
        in_specs=[SMEM, SMEM, VMEM, VMEM, VMEM, ANY, ANY, ANY],
        out_specs=[ANY] * len(shapes),
        scratch_shapes=[pltpu.VMEM(a.shape, BF16) for a in (d_merged, w_qkv, w_out)]
        + [pltpu.VMEM(s, BF16) for s in shapes]
        + [
            pltpu.VMEM((row_count, model_width), F32),
            pltpu.VMEM((model_width, row_count), BF16),
            pltpu.VMEM((model_width, row_count + LANES), BF16),
            pltpu.VMEM((row_count, inner), BF16),
            pltpu.VMEM((row_count + LANES, model_width), BF16),
            pltpu.VMEM((8, model_width), F32),
            pltpu.VMEM((row_count, LANES), F32),
            pltpu.VMEM((row_count, row_count), BF16),
            pltpu.SemaphoreType.DMA((loads,)),
            pltpu.SemaphoreType.DMA((len(shapes),)),
        ],
        compiler_params=pltpu.CompilerParams(vmem_limit_bytes=58 * 2**20),
        cost_estimate=SMALL,
    )(rank, window_live, window_index, patches, gain, d_merged, w_qkv, w_out)


def run_backward(packed, probs, d_context, heights):
    pairs, _, inner, block = packed.shape
    return pl.pallas_call(
        backward_kernel,
        out_shape=[jax.ShapeDtypeStruct((h, pairs * block), BF16) for h in heights],
        grid=(pairs,),
        in_specs=[
            pl.BlockSpec((1, 3, inner, block), lambda n: (n, 0, 0, 0)),
            pl.BlockSpec((1, HEADS, block, block), lambda n: (n, 0, 0, 0)),
            pl.BlockSpec((1, inner, block), lambda n: (n, 0, 0)),
        ],
        out_specs=[pl.BlockSpec((h, block), lambda n: (0, n)) for h in heights],
        compiler_params=pltpu.CompilerParams(vmem_limit_bytes=56 * 2**20),
        cost_estimate=SMALL,
    )(packed, probs, d_context)


def on_device(patches, window_index, window_live, d_merged, w_qkv, w_out, merge_gain):
    model_width = patches.shape[1]
    inner = w_out.shape[0]
    ranks = lax.axis_size("dp")
    rank = lax.axis_index("dp")
    bits = ranks.bit_length() - 2
    (
        merged, packed, probs, d_context, context, norm_keep, norm_send, att_keep, att_send
    ) = run_forward(
        rank.reshape(1), window_live, window_index, patches,
        merge_gain, d_merged, w_qkv.T, w_out, ranks // 2,
    )

    def swap(array):
        return lax.ppermute(array, "dp", flip_pairs(ranks, 0))

    along = list(range(1, bits + 1))
    by_x = along + ["vis"]
    by_y = along[bits // 2:] + along[:bits // 2] + ["vis"]
    early, late, last = 8 * LANES, 15 * LANES, 3 * inner

    got = [swap(context), swap(att_send), swap(norm_send)]
    d_first, d_last = run_backward(packed, probs, d_context, (early, last - early))
    got, (d_first, d_last) = together(got, [d_first, d_last])
    context_got, att_got, norm_got = got
    first_got = swap(d_first)
    norm = (norm_keep, norm_got)

    ((sent, kept),) = product(
        (att_keep, att_got), (context, context_got), [((0, inner), by_x[0])], inner
    )
    sum_out = Sum(None, by_x)
    sum_out.first(sent, kept)

    (first_got,), (d_last, sum_out.kept) = together([first_got], [d_last, sum_out.kept])
    last_got = swap(d_last)
    ((sent, kept),) = product(norm, (d_first, first_got), [((0, early), by_y[0])])
    sum_1 = Sum(None, by_y)
    sum_1.first(sent, kept)

    (last_got,), (sum_1.kept,) = together([last_got], [sum_1.kept])
    (sent_2, kept_2), (sent_3, kept_3) = product(
        norm, (d_last, last_got), [((0, late - early), by_x[0]), ((late - early, last - early), by_y[0])]
    )

    kept_2, sent_2 = sum_out.after([kept_2, sent_2])
    kept_3, sent_3 = sum_1.after([kept_3, sent_3])
    sum_2, sum_3 = Sum(None, by_x), Sum(None, by_y)
    sum_2.first(sent_2, kept_2)
    sum_3.first(sent_3, kept_3)
    for _ in range(bits - 1):
        sum_out.step()
        sum_1.step()
    spread_1 = Spread([sum_out.whole(), sum_1.whole()])
    for _ in range(bits - 1):
        sum_2.step()
        sum_3.step()
    wholes = [sum_2.whole(), sum_3.whole()]
    spread_1.got, wholes = together(spread_1.got, wholes)
    spread_2 = Spread(wholes)
    total, total_late = spread_1.total(), spread_2.total()
    width = ceil_to(inner + 1, LANES)
    total_out, total_1 = total[:, :width], total[:, width:]
    total_qkv = jnp.concatenate([total_1, total_late], axis=-1)
    return (merged, total_qkv, total_out[:, :inner].T, total_out[:, inner])


def solution(mesh):
    in_specs = (
        P(("dp", "vis"), None),
        P(("dp", "vis"), None),
        P(("dp", "vis"), None),
        P(("dp", "vis"), None),
        P(),
        P(),
        P(),
    )
    out_specs = (
        P(("dp", "vis"), None),
        P(("dp", "vis"), None),
        P(None, ("dp", "vis")),
        P(("dp", "vis")),
    )
    return jax.shard_map(
        on_device, mesh=mesh, in_specs=in_specs, out_specs=out_specs, check_vma=False
    )
```

```python
import functools

import jax
import jax.numpy as jnp
from jax import lax
from jax.experimental import pallas as pl
from jax.experimental.pallas import tpu as pltpu
from jax.sharding import PartitionSpec as P

HEADS = 12
SIDE_FORWARD, SIDE_BACKWARD = 12, 12
JOIN = 4
PAIR = 2
LANES = 128
TILE = 256
EPSILON = 1e-06
NEGATIVE = -1e30
F32 = jnp.float32
BF16 = jnp.bfloat16


def ceil_to(size, step):
    return -(-size // step) * step


def dot(left, right, left_axis=1, right_axis=0):
    return lax.dot_general(
        left, right, (((left_axis,), (right_axis,)), ((), ())), preferred_element_type=F32
    )


def tiles(width, step=TILE):
    return [(at, min(step, width - at)) for at in range(0, width, step)]


def alive_of(place, live_first, live_second, group):
    limit = jnp.where((place // group) % PAIR == 0, live_first, live_second)
    return (place % group) * JOIN < limit


def forward_kernel(
    rank_ref, live_ref, index_ref, patches_ref, gain_ref, cot_hbm, w_qkv_hbm, w_out_hbm,
    merged_hbm, packed_hbm, probs_hbm, d_context_hbm, context_hbm,
    norm_keep_hbm, norm_send_hbm, att_keep_hbm, att_send_hbm,
    cot_ref, w_qkv_ref, w_out_ref,
    merged_ref, packed_ref, probs_ref, d_context_ref, context_ref,
    norm_keep_ref, norm_send_ref, att_keep_ref, att_send_ref,
    rows_ref, norm_ref, turned_ref, upright_ref, d_att_ref, gain_sum_ref, place_ref, chosen_ref,
    in_sems, out_sems,
):
    row_count, model_width = patches_ref.shape
    inner = w_out_ref.shape[0]
    head_width = inner // HEADS
    slots = live_ref.shape[1]
    win_rows = row_count // slots
    group = win_rows // JOIN
    block = PAIR * win_rows
    strip = PAIR * group
    pairs = slots // PAIR
    scale = head_width ** (-0.5)
    outs = {}

    parts = tiles(3 * inner, inner // 2)
    loads = [
        pltpu.make_async_copy(
            w_qkv_hbm.at[pl.ds(at, size)], w_qkv_ref.at[pl.ds(at, size)], in_sems.at[n]
        )
        for n, (at, size) in enumerate(parts)
    ]
    load_out = pltpu.make_async_copy(w_out_hbm, w_out_ref, in_sems.at[len(parts)])
    load_cot = pltpu.make_async_copy(cot_hbm, cot_ref, in_sems.at[len(parts) + 1])
    for load in loads + [load_out, load_cot]:
        load.start()

    def give(n, source, target):
        outs[n] = pltpu.make_async_copy(source, target, out_sems.at[n])
        outs[n].start()

    def by_core(source, keep, send):
        half, rank_rows, _ = keep.shape
        core, chip = rank_ref[0] & 1, rank_ref[0] >> 1
        for rank in range(2 * half):
            piece = source[rank * rank_rows:(rank + 1) * rank_rows, :]

            @pl.when(core == rank % 2)
            def _():
                keep[chip ^ (rank // 2)] = piece

            @pl.when(core != rank % 2)
            def _():
                send[chip ^ (rank // 2)] = piece

    places = jnp.broadcast_to(index_ref[...].astype(F32), (LANES, row_count))
    place_ref[...] = places.T
    raster = lax.broadcasted_iota(jnp.int32, (strip, row_count), 1)
    for pair in range(pairs):
        for turn in range(JOIN):
            at = pair * block + turn * strip
            place = place_ref[pl.ds(pair * block + turn, strip, stride=JOIN), :]
            found = raster == place[:, :1].astype(jnp.int32)
            chosen_ref[at:at + strip, :] = jnp.where(found, 1.0, 0.0).astype(BF16)
    for at, size in tiles(model_width):
        rows_ref[:, at:at + size] = dot(chosen_ref[...], patches_ref[:, at:at + size])

    for pair in range(pairs):
        here = slice(pair * block, (pair + 1) * block)
        rows = rows_ref[here, :]
        power = jnp.mean(rows * rows, axis=1, keepdims=True)
        normed = (rows * lax.rsqrt(power + EPSILON)).astype(BF16)
        norm_ref[:, here] = normed.T
    by_core(norm_ref, norm_keep_ref, norm_send_ref)
    give(0, norm_keep_ref, norm_keep_hbm)
    give(1, norm_send_ref, norm_send_hbm)

    for load, (first, height) in zip(loads, parts):
        load.wait()
        for at, size in tiles(height):
            at += first
            found = dot(w_qkv_ref[at:at + size, :], norm_ref[...]).astype(BF16)
            part, at = at // inner, at % inner
            for pair in range(pairs):
                packed_ref[pair, part, at:at + size, :] = found[:, pair * block:(pair + 1) * block]
    give(2, packed_ref, packed_hbm)

    @pl.loop(0, pairs, unroll=2)
    def _(pair):
        here = pl.ds(pl.multiple_of(pair * block, block), block)
        key_at = lax.broadcasted_iota(jnp.int32, (block, block), 0)
        query_at = lax.broadcasted_iota(jnp.int32, (block, block), 1)
        allowed = alive_of(key_at, live_ref[0, PAIR * pair], live_ref[0, PAIR * pair + 1], group)
        allowed = allowed & ((key_at // group) % PAIR == (query_at // group) % PAIR)
        for first in range(0, HEADS, SIDE_FORWARD):
            spans = [
                slice(head * head_width, (head + 1) * head_width)
                for head in range(first, first + SIDE_FORWARD)
            ]
            scores = [
                dot(packed_ref[pair, 1, span, :], packed_ref[pair, 0, span, :], 0, 0)
                for span in spans
            ]
            probs = []
            for one in scores:
                one = jnp.where(allowed, one, NEGATIVE)
                grown = jnp.exp((one - jnp.max(one, axis=0, keepdims=True)) * scale)
                one = grown * (1.0 / jnp.sum(grown, axis=0, keepdims=True))
                probs.append(one.astype(BF16))
            found = [dot(packed_ref[pair, 2, span, :], one) for span, one in zip(spans, probs)]
            for n, span in enumerate(spans):
                probs_ref[pair, first + n] = probs[n]
                context_ref[span, here] = found[n].astype(BF16)

    give(3, probs_ref, probs_hbm)
    give(4, context_ref, context_hbm)
    for pair in range(pairs):
        here = slice(pair * block, (pair + 1) * block)
        upright_ref[here, :] = context_ref[:, here].T
    load_out.wait()
    for at, size in tiles(model_width):
        rows_ref[:, at:at + size] += dot(upright_ref[...], w_out_ref[:, at:at + size])

    gain_sum_ref[...] = jnp.zeros_like(gain_sum_ref)
    load_cot.wait()

    for pair in range(pairs):
        row_at = lax.broadcasted_iota(jnp.int32, (strip, 1), 0)
        alive = alive_of(row_at, live_ref[0, PAIR * pair], live_ref[0, PAIR * pair + 1], group)
        alive = jnp.where(alive, 1.0, 0.0)
        gain = gain_ref[...].reshape(1, model_width)
        out_rows = slice(pair * strip, (pair + 1) * strip)
        for turn in range(JOIN):
            here = slice(pair * block + turn * strip, pair * block + (turn + 1) * strip)
            columns = slice(turn * model_width, (turn + 1) * model_width)
            attended = rows_ref[here, :]
            power = jnp.mean(attended * attended, axis=1, keepdims=True)
            inverse = lax.rsqrt(power + EPSILON)
            normalized = attended * inverse
            merged_ref[out_rows, columns] = (normalized * gain * alive).astype(BF16)
            grad_rows = cot_ref[out_rows, columns].astype(F32) * alive
            crossed = grad_rows * normalized
            gain_sum_ref[...] += jnp.sum(crossed.reshape(strip // 8, 8, model_width), axis=0)
            mean = jnp.mean(crossed * gain, axis=1, keepdims=True)
            d_att_ref[here, :] = (inverse * (grad_rows * gain - normalized * mean)).astype(BF16)

    give(5, merged_ref, merged_hbm)
    total = jnp.sum(gain_sum_ref[...], axis=0, keepdims=True)
    high = total.astype(BF16).astype(F32)
    at_row = lax.broadcasted_iota(jnp.int32, (LANES, model_width), 0)
    tail = jnp.where(at_row == 0, high, jnp.where(at_row == 1, total - high, 0.0))
    d_att_ref[row_count:, :] = tail.astype(BF16)

    for at, size in tiles(row_count + LANES, LANES):
        turned_ref[:, at:at + size] = d_att_ref[at:at + size, :].T
    by_core(turned_ref, att_keep_ref, att_send_ref)
    give(6, att_keep_ref, att_keep_hbm)
    give(7, att_send_ref, att_send_hbm)

    for at, size in tiles(inner):
        found = dot(w_out_ref[at:at + size, :], turned_ref[:, :row_count]).astype(BF16)
        for pair in range(pairs):
            d_context_ref[pair, at:at + size, :] = found[:, pair * block:(pair + 1) * block]
    give(8, d_context_ref, d_context_hbm)
    for n in sorted(outs):
        outs[n].wait()


def backward_kernel(packed_ref, probs_ref, d_context_ref, *outs):
    _, heads, block, _ = probs_ref.shape
    inner = d_context_ref.shape[1]
    head_width = inner // heads
    scale = head_width ** (-0.5)

    def put(at, value):
        value = value.astype(BF16)
        for ref in outs:
            taken = max(0, min(ref.shape[0] - at, value.shape[0]))
            if taken > 0:
                ref[at:at + taken, :] = value[:taken]
                value = value[taken:]
                at += taken
            at -= ref.shape[0]

    for first in range(0, heads, SIDE_BACKWARD):
        together = range(first, first + SIDE_BACKWARD)
        spans = [slice(head * head_width, (head + 1) * head_width) for head in together]
        probs = [probs_ref[0, head] for head in together]
        d_probs = [
            dot(packed_ref[0, 2, span, :], d_context_ref[0, span, :], 0, 0) for span in spans
        ]
        d_scores = []
        for low, one in zip(probs, d_probs):
            exact = low.astype(F32)
            inside = jnp.sum(one * exact, axis=0, keepdims=True)
            d_scores.append((exact * (one - inside) * scale).astype(BF16))
        founds = (
            [dot(packed_ref[0, 1, span, :], one) for span, one in zip(spans, d_scores)],
            [dot(packed_ref[0, 0, span, :], one, 1, 1) for span, one in zip(spans, d_scores)],
            [dot(d_context_ref[0, span, :], one, 1, 1) for span, one in zip(spans, probs)],
        )
        for n, found in enumerate(founds):
            for span, one in zip(spans, found):
                put(n * inner + span.start, one)


def product_kernel(keep_ref, other_ref, right_ref, right_other_ref, *outs, pieces, extra_at):
    half, rank_rows, _ = keep_ref.shape
    depth = right_ref.shape[1]
    whole = rank_rows % 16 == 0
    for groups in [list(range(half))] if whole else [[g] for g in range(half)]:
        lefts = []
        for ref in (keep_ref, other_ref):
            rows = [ref[g] for g in groups]
            lefts.append(jnp.concatenate(rows, axis=0) if whole else rows[0])
        number = 0
        for (first, last), lists in pieces:
            def put(total, at):
                for n, g in enumerate(groups):
                    for ref, held in zip(outs[number:], lists):
                        if g in held:
                            ref[held.index(g), :, at:at + total.shape[1]] = total[
                                n * rank_rows:(n + 1) * rank_rows
                            ].astype(BF16)

            for at, size in tiles(last - first, 2 * TILE):
                span = slice(first + at, first + at + size)
                total = dot(lefts[0][:, :depth], right_ref[span, :], 1, 1)
                total += dot(lefts[1][:, :depth], right_other_ref[span, :], 1, 1)
                put(total, at)
            if extra_at is not None:
                column = lax.broadcasted_iota(jnp.int32, (LANES, LANES), 1)
                ones = jnp.where(column == extra_at % LANES, 1.0, 0.0).astype(BF16)
                total = dot(lefts[0][:, depth:], ones) + dot(lefts[1][:, depth:], ones)
                put(total[:, extra_at % LANES:], extra_at)
            number += len(lists)


def product(left, right, pieces, extra_at=None):
    keep, other = left
    half, rank_rows, _ = keep.shape
    taken, shapes, counts = [], [], []
    for (first, last), axis in pieces:
        sent = [] if axis == "vis" else [g for g in range(half) if (g >> (axis - 1)) & 1]
        lists = [held for held in (sent, [g for g in range(half) if g not in sent]) if held]
        width = last - first if extra_at is None else ceil_to(last - first + 1, LANES)
        taken.append(((first, last), lists))
        shapes += [jax.ShapeDtypeStruct((len(held), rank_rows, width), BF16) for held in lists]
        counts.append(len(lists))
    found = pl.pallas_call(
        functools.partial(product_kernel, pieces=taken, extra_at=extra_at),
        out_shape=shapes,
        in_specs=[VMEM] * 4,
        out_specs=[VMEM] * len(shapes),
        compiler_params=pltpu.CompilerParams(vmem_limit_bytes=24 * 2**20),
        cost_estimate=SMALL,
    )(keep, other, *right)
    return [found[sum(counts[:n]):sum(counts[:n + 1])] for n in range(len(counts))]


def flip_pairs(size, bit):
    return [(i, i ^ (1 << bit)) for i in range(size)]


def pick(array, place, axis):
    return lax.dynamic_index_in_dim(array, place, axis, keepdims=False)


def together(arrays, others):
    found = lax.optimization_barrier((*arrays, *others))
    return list(found[:len(arrays)]), list(found[len(arrays):])


class Sum:
    def __init__(self, kept, order):
        self.ranks = lax.axis_size("dp")
        self.order = list(order)
        self.left = [b for b in range(self.ranks.bit_length() - 2, 0, -1)]
        self.kept, self.got = kept, []

    def first(self, sent, kept):
        self.arrived(lax.ppermute(sent, "dp", flip_pairs(self.ranks, self.order[0])), kept)

    def arrived(self, got, kept):
        bit, *self.order = self.order
        self.left.remove(bit)
        shape = (2,) * len(self.left) + kept.shape[1:]
        self.kept, self.got = kept.reshape(shape), [got.reshape(shape)]

    def after(self, others):
        self.got, others = together(self.got, others)
        return others

    def step(self):
        axis, *self.order = self.order
        terms = [self.kept, *self.got]
        if axis == "vis":
            layers, layer = lax.axis_size("vis"), lax.axis_index("vis")
            whole = total_of(terms).astype(BF16)
            places = 2 ** len(self.left)
            shards = whole.reshape(places, layers, -1, whole.shape[-1])
            self.kept = pick(shards, layer, 1)
            self.got = []
            for k in range(1, layers):
                pairs = [(i, (i + k) % layers) for i in range(layers)]
                sent = pick(shards, (layer + k) % layers, 1)
                self.got.append(lax.ppermute(sent, "vis", pairs))
            return
        sent = self.part(axis)
        self.got = [lax.ppermute(sent, "dp", flip_pairs(self.ranks, axis))]

    def part(self, axis):
        shape = (2,) * len(self.left) + self.kept.shape[-2:]
        at = self.left.index(axis)
        terms = [one.reshape(shape) for one in (self.kept, *self.got)]
        self.kept, sent = [
            total_of([lax.index_in_dim(one, n, at, keepdims=False) for one in terms]).astype(BF16)
            for n in range(2)
        ]
        self.left.remove(axis)
        return sent

    def total(self):
        return total_of([self.kept, *self.got])

    def whole(self):
        return self.total().astype(BF16).reshape(self.kept.shape[-2:])


def total_of(terms):
    total = terms[0].astype(F32)
    for one in terms[1:]:
        total = total + one.astype(F32)
    return total


class Spread(Sum):
    def __init__(self, wholes):
        layers, layer = lax.axis_size("vis"), lax.axis_index("vis")
        shards = [whole.reshape(layers, -1, whole.shape[-1]) for whole in wholes]

        def row_of(k):
            place = (layer + k) % layers
            return jnp.concatenate([pick(one, place, 0) for one in shards], axis=-1)

        self.kept = row_of(0)
        self.got = []
        for k in range(1, layers):
            pairs = [(i, (i + k) % layers) for i in range(layers)]
            self.got.append(lax.ppermute(row_of(k), "vis", pairs))


VMEM = pl.BlockSpec(memory_space=pltpu.VMEM)
SMEM = pl.BlockSpec(memory_space=pltpu.SMEM)
ANY = pl.BlockSpec(memory_space=pl.ANY)


SMALL = pl.CostEstimate(flops=1, bytes_accessed=1, transcendentals=0)


def run_forward(rank, window_live, window_index, patches, gain, d_merged, w_qkv, w_out, half):
    row_count, model_width = patches.shape
    inner = w_out.shape[0]
    slots = window_live.shape[1]
    block = PAIR * row_count // slots
    pairs = slots // PAIR
    rank_rows = model_width // (2 * half)
    shapes = [
        d_merged.shape,
        (pairs, 3, inner, block),
        (pairs, HEADS, block, block),
        (pairs, inner, block),
        (inner, row_count),
        (half, rank_rows, row_count),
        (half, rank_rows, row_count),
        (half, rank_rows, row_count + LANES),
        (half, rank_rows, row_count + LANES),
    ]
    loads = 2 + len(tiles(3 * inner, inner // 2))
    return pl.pallas_call(
        forward_kernel,
        out_shape=[jax.ShapeDtypeStruct(s, BF16) for s in shapes],
        in_specs=[SMEM, SMEM, VMEM, VMEM, VMEM, ANY, ANY, ANY],
        out_specs=[ANY] * len(shapes),
        scratch_shapes=[pltpu.VMEM(a.shape, BF16) for a in (d_merged, w_qkv, w_out)]
        + [pltpu.VMEM(s, BF16) for s in shapes]
        + [
            pltpu.VMEM((row_count, model_width), F32),
            pltpu.VMEM((model_width, row_count), BF16),
            pltpu.VMEM((model_width, row_count + LANES), BF16),
            pltpu.VMEM((row_count, inner), BF16),
            pltpu.VMEM((row_count + LANES, model_width), BF16),
            pltpu.VMEM((8, model_width), F32),
            pltpu.VMEM((row_count, LANES), F32),
            pltpu.VMEM((row_count, row_count), BF16),
            pltpu.SemaphoreType.DMA((loads,)),
            pltpu.SemaphoreType.DMA((len(shapes),)),
        ],
        compiler_params=pltpu.CompilerParams(vmem_limit_bytes=58 * 2**20),
        cost_estimate=SMALL,
    )(rank, window_live, window_index, patches, gain, d_merged, w_qkv, w_out)


def run_backward(packed, probs, d_context, heights):
    pairs, _, inner, block = packed.shape
    return pl.pallas_call(
        backward_kernel,
        out_shape=[jax.ShapeDtypeStruct((h, pairs * block), BF16) for h in heights],
        grid=(pairs,),
        in_specs=[
            pl.BlockSpec((1, 3, inner, block), lambda n: (n, 0, 0, 0)),
            pl.BlockSpec((1, HEADS, block, block), lambda n: (n, 0, 0, 0)),
            pl.BlockSpec((1, inner, block), lambda n: (n, 0, 0)),
        ],
        out_specs=[pl.BlockSpec((h, block), lambda n: (0, n)) for h in heights],
        compiler_params=pltpu.CompilerParams(vmem_limit_bytes=56 * 2**20),
        cost_estimate=SMALL,
    )(packed, probs, d_context)


def on_device(patches, window_index, window_live, d_merged, w_qkv, w_out, merge_gain):
    model_width = patches.shape[1]
    inner = w_out.shape[0]
    ranks = lax.axis_size("dp")
    rank = lax.axis_index("dp")
    bits = ranks.bit_length() - 2
    (
        merged, packed, probs, d_context, context, norm_keep, norm_send, att_keep, att_send
    ) = run_forward(
        rank.reshape(1), window_live, window_index, patches,
        merge_gain, d_merged, w_qkv.T, w_out, ranks // 2,
    )

    def swap(array):
        return lax.ppermute(array, "dp", flip_pairs(ranks, 0))

    along = list(range(1, bits + 1))
    by_x = along + ["vis"]
    by_y = along[bits // 2:] + along[:bits // 2] + ["vis"]
    early, late, last = 8 * LANES, 15 * LANES, 3 * inner

    got = [swap(context), swap(att_send), swap(norm_send)]
    d_first, d_last = run_backward(packed, probs, d_context, (early, last - early))
    got, (d_first, d_last) = together(got, [d_first, d_last])
    context_got, att_got, norm_got = got
    first_got = swap(d_first)
    norm = (norm_keep, norm_got)

    ((sent, kept),) = product(
        (att_keep, att_got), (context, context_got), [((0, inner), by_x[0])], inner
    )
    sum_out = Sum(None, by_x)
    sum_out.first(sent, kept)

    (first_got,), (d_last, sum_out.kept) = together([first_got], [d_last, sum_out.kept])
    last_got = swap(d_last)
    ((sent, kept),) = product(norm, (d_first, first_got), [((0, early), by_y[0])])
    sum_1 = Sum(None, by_y)
    sum_1.first(sent, kept)

    (last_got,), (sum_1.kept,) = together([last_got], [sum_1.kept])
    (sent_2, kept_2), (sent_3, kept_3) = product(
        norm, (d_last, last_got), [((0, late - early), by_x[0]), ((late - early, last - early), by_y[0])]
    )

    kept_2, sent_2 = sum_out.after([kept_2, sent_2])
    kept_3, sent_3 = sum_1.after([kept_3, sent_3])
    sum_2, sum_3 = Sum(None, by_x), Sum(None, by_y)
    sum_2.first(sent_2, kept_2)
    sum_3.first(sent_3, kept_3)
    for _ in range(bits - 1):
        sum_out.step()
        sum_1.step()
    spread_1 = Spread([sum_out.whole(), sum_1.whole()])
    for _ in range(bits - 1):
        sum_2.step()
        sum_3.step()
    wholes = [sum_2.whole(), sum_3.whole()]
    spread_1.got, wholes = together(spread_1.got, wholes)
    spread_2 = Spread(wholes)
    total, total_late = spread_1.total(), spread_2.total()
    width = ceil_to(inner + 1, LANES)
    total_out, total_1 = total[:, :width], total[:, width:]
    total_qkv = jnp.concatenate([total_1, total_late], axis=-1)
    return (merged, total_qkv, total_out[:, :inner].T, total_out[:, inner])


def solution(mesh):
    in_specs = (
        P(("dp", "vis"), None),
        P(("dp", "vis"), None),
        P(("dp", "vis"), None),
        P(("dp", "vis"), None),
        P(),
        P(),
        P(),
    )
    out_specs = (
        P(("dp", "vis"), None),
        P(("dp", "vis"), None),
        P(None, ("dp", "vis")),
        P(("dp", "vis")),
    )
    return jax.shard_map(
        on_device, mesh=mesh, in_specs=in_specs, out_specs=out_specs, check_vma=False
    )
```
